512 devices in a mesh: row: 16 (over y, x_hi, core), col: 32 (over x_lo, z).
Axes of the slice: x: 4 (x_hi: 2, x_lo: 2; x = x_hi * 2 + x_lo), y: 4, z: 16, core: 2. Of those that a mesh axis runs over, the one named last changes fastest.
Arguments:
- pair: bfloat16 [512, 512, 128], P('row', 'col'), may hold values from -6 to 6
- pair_mask: int32 [512, 512], P('row', 'col'), may hold values 0 or 1
- norm_gain: float32 [128], replicated, may hold values from 0.5 to 1.5
- norm_bias: float32 [128], replicated, may hold values from -3 to 3
- w_a_gate: bfloat16 [128, 128], replicated, may hold values from -0.5 to 0.5
- w_a_proj: bfloat16 [128, 128], replicated, may hold values from -0.5 to 0.5
- w_b_gate: bfloat16 [128, 128], replicated, may hold values from -0.5 to 0.5
- w_b_proj: bfloat16 [128, 128], replicated, may hold values from -0.5 to 0.5
- w_gate: bfloat16 [128, 128], replicated, may hold values from -0.5 to 0.5
- out_gain: float32 [128], replicated, may hold values from 0.5 to 1.5
- out_bias: float32 [128], replicated, may hold values from -3 to 3
- w_out: bfloat16 [128, 128], replicated, may hold values from -0.5 to 0.5
Outputs:
- update: bfloat16 [512, 512, 128], P('row', 'col')
The draws below stay inside these ranges and needn't reach their ends.
All inputs are finite; a program needn't handle non-finite values. No bound on the sum of `pair_mask` on one device may be relied on, other than what follows from the above.
Results may differ from the reference program's by a relative error of at most 0.0054.
Values may be sent and summed in bfloat16 or wider, within the bound.
A program may use at most 64 MiB of HBM per device.

```python
import jax
import jax.numpy as jnp
from jax import lax

C = 128
H = 128
N = 512


def plant(entries, stream_key, least, largest):
    place = [jax.random.randint(jax.random.fold_in(stream_key, axis), (), 0, length) for axis, length in enumerate(entries.shape)]
    main_axis = entries.shape.index(max(entries.shape))
    beside = place[:main_axis] + [(place[main_axis] + 1) % entries.shape[main_axis]] + place[main_axis + 1:]
    return entries.at[tuple(place)].set(least).at[tuple(beside)].set(largest)


def block_scale(own_key, shape, split, smallest, top_value):
    def one(axis_at, shards_of):
        heights = jax.random.uniform(jax.random.fold_in(jax.random.fold_in(own_key, 6), axis_at), (shards_of,), jnp.float32, smallest / len(split), top_value / len(split))
        return jnp.repeat(jnp.exp(heights), shape[axis_at] // shards_of).reshape((-1,) + (1,) * (len(shape) - axis_at - 1))

    factor_of = one(*split[0])
    for cut in split[1:]:
        factor_of = factor_of * one(*cut)
    return factor_of


def bell_draw(own_key, shape, deviation, limit, shards=(), kind=jnp.bfloat16):
    values = deviation * jax.random.normal(own_key, shape, jnp.float32)
    if shards:
        values = values * block_scale(own_key, shape, shards, -0.22, 0.18)
    return jnp.clip(values, -limit, limit).astype(kind)


def setup_inputs(seed: int = 0) -> dict:
    keys = jax.random.split(jax.random.key(seed), 13)
    pair = bell_draw(keys[0], (N, N, C), 1.0, 6.0, ((0, 16), (1, 32)))
    pair_mask = plant((jax.random.randint(keys[1], (N, N), 0, 8) < 7).astype(jnp.int32), jax.random.fold_in(keys[1], 1), 0, 1)
    norm_gain = jnp.clip(jax.random.uniform(keys[2], (C,), jnp.float32, 0.5, 1.5), 0.5, 1.5)
    norm_bias = bell_draw(keys[3], (C,), 0.5, 3.0, (), jnp.float32)
    w_a_gate = bell_draw(keys[4], (C, H), C ** -0.5, 0.5)
    w_a_proj = bell_draw(keys[5], (C, H), C ** -0.5, 0.5)
    w_b_gate = bell_draw(keys[6], (C, H), C ** -0.5, 0.5)
    w_b_proj = bell_draw(keys[7], (C, H), C ** -0.5, 0.5)
    w_gate = bell_draw(keys[8], (C, C), C ** -0.5, 0.5)
    out_gain = jnp.clip(jax.random.uniform(keys[9], (H,), jnp.float32, 0.5, 1.5), 0.5, 1.5)
    out_bias = bell_draw(keys[10], (H,), 0.5, 3.0, (), jnp.float32)
    w_out = bell_draw(keys[11], (H, C), H ** -0.5, 0.5)
    return {"pair": pair, "pair_mask": pair_mask, "norm_gain": norm_gain, "norm_bias": norm_bias, "w_a_gate": w_a_gate, "w_a_proj": w_a_proj, "w_b_gate": w_b_gate, "w_b_proj": w_b_proj, "w_gate": w_gate, "out_gain": out_gain, "out_bias": out_bias, "w_out": w_out}


def layer_norm(values, gain, bias):
    mean = lax.optimization_barrier(jnp.mean(values, axis=-1, keepdims=True))
    centred = values - mean
    variance = lax.optimization_barrier(jnp.mean(centred * centred, axis=-1, keepdims=True))
    return centred * lax.rsqrt(variance + 1e-05) * gain + bias

def reference(pair, pair_mask, norm_gain, norm_bias, w_a_gate, w_a_proj, w_b_gate, w_b_proj, w_gate, out_gain, out_bias, w_out):
    count = pair.shape[0]
    width = pair.shape[2]
    normed = layer_norm(pair.astype(jnp.float32), norm_gain, norm_bias).astype(jnp.bfloat16)
    flat = normed.reshape(count * count, width)
    mask_col = pair_mask.astype(jnp.float32).reshape(count * count, 1)

    def project(weight):
        return jnp.dot(flat, weight, preferred_element_type=jnp.float32)
    left = (mask_col * jax.nn.sigmoid(project(w_a_gate)) * project(w_a_proj)).astype(jnp.bfloat16)
    right = (mask_col * jax.nn.sigmoid(project(w_b_gate)) * project(w_b_proj)).astype(jnp.bfloat16)
    gate = jax.nn.sigmoid(project(w_gate))
    hidden = left.shape[1]
    left = left.reshape(count, count, hidden).astype(jnp.float32)
    right = right.reshape(count, count, hidden).astype(jnp.float32)
    contracted = jnp.einsum('ikc,jkc->ijc', left, right, precision=lax.Precision.HIGHEST)
    normed_out = layer_norm(contracted, out_gain, out_bias).astype(jnp.bfloat16)
    result = gate * jnp.dot(normed_out.reshape(count * count, hidden), w_out, preferred_element_type=jnp.float32)
    return result.astype(jnp.bfloat16).reshape(count, count, width)
```

```python
import jax
import jax.numpy as jnp
from jax import lax
from jax.experimental import pallas as pl
from jax.experimental.pallas import tpu as pltpu
from jax.sharding import PartitionSpec as P

MESH = pl.DeviceIdType.MESH
F32, BF16 = jnp.float32, jnp.bfloat16
NZ, NX, NY = 16, 4, 4
FAR_FIRST = (8, 7, 9, 6, 10, 5, 11, 4, 12, 3, 13, 2, 14, 1, 15)
PLANE = tuple((dy, dx) for dy in (2, 1, 3, 0) for dx in (2, 1, 3, 0) if dy or dx)
ALONG_X = (2, 1, 3)
NT = (((1,), (1,)), ((), ()))
TN = (((0,), (0,)), ((), ()))


def swap_blocks(arrays):
    arrays = list(arrays)
    lane = lax.broadcasted_iota(jnp.int32, arrays[0].shape, 1)
    for bit in range(3):
        step = 1 << bit
        upper = ((lane // 16) // step) % 2 == 1
        for a in range(8):
            if not a & step:
                low, high = arrays[a], arrays[a | step]
                arrays[a] = jnp.where(upper, pltpu.roll(high, 16 * step, 1), low)
                arrays[a | step] = jnp.where(upper, high, pltpu.roll(low, 128 - 16 * step, 1))
    return arrays


def kernel(
    pair_hbm, mask_hbm, norm_gain_hbm, norm_bias_hbm, w_a_gate_hbm, w_a_proj_hbm, w_b_gate_hbm, w_b_proj_hbm,
    w_gate_hbm, out_gain_hbm, out_bias_hbm, w_out_hbm,
    out_ref,
    pair, mask, norm_gain, norm_bias, w_a_gate, w_a_proj, w_b_gate, w_b_proj, w_gate, out_gain, out_bias, w_out,
    normed, gate, z_send, z_recv, turned, edges, shared, left_all, right_all, product, product_x, turned_back,
    back_send, back_recv,
    in_sem, z_ss, z_rs, core_ss, core_rs, right_ss, right_rs, left_ss, left_rs, x_ss, x_rs, back_ss, back_rs, local_sem,
):
    row, col = lax.axis_index("row"), lax.axis_index("col")
    y, core = row // 4, row % 2
    x = ((row // 2) % 2) * 2 + col // 16
    z = col % 16

    def device(y, x, core, z):
        return {"row": y * 4 + (x // 2) * 2 + core, "col": (x % 2) * 16 + z}

    z_peers = [device(y, x, core, (z + d) % NZ) for d in FAR_FIRST]
    plane_peers = [device((y + dy) % NY, (x + dx) % NX, core, z) for dy, dx in PLANE]
    other_core = device(y, x, 1 - core, z)
    x_other_core = [device(y, (x + dx) % NX, 1 - core, z) for dx in ALONG_X]
    barrier = pltpu.get_barrier_semaphore()
    peers = z_peers + plane_peers + [other_core] + x_other_core
    for peer in peers:
        pl.semaphore_signal(barrier, inc=1, device_id=peer, device_id_type=MESH)

    hbm = (pair_hbm, mask_hbm, norm_gain_hbm, norm_bias_hbm, w_a_gate_hbm, w_a_proj_hbm, w_b_gate_hbm, w_b_proj_hbm,
           w_gate_hbm, out_gain_hbm, out_bias_hbm, w_out_hbm)
    vmem = (pair, mask, norm_gain, norm_bias, w_a_gate, w_a_proj, w_b_gate, w_b_proj, w_gate, out_gain, out_bias, w_out)
    loads = [pltpu.make_async_copy(src, dst, in_sem.at[n]) for n, (src, dst) in enumerate(zip(hbm, vmem))]
    for load in loads:
        load.start()
    for load in loads:
        load.wait()

    values = pair[...].astype(F32).reshape(512, 128)
    centred = values - jnp.mean(values, axis=1, keepdims=True)
    variance = jnp.mean(centred * centred, axis=1, keepdims=True)
    normed[...] = (centred * lax.rsqrt(variance + 1e-05) * norm_gain[...] + norm_bias[...]).astype(BF16)

    at_col = lax.broadcasted_iota(jnp.int32, (16, 512), 1) % 16 == lax.broadcasted_iota(jnp.int32, (16, 512), 0)
    at_row = lax.broadcasted_iota(jnp.int32, (32, 512), 1) // 16 == lax.broadcasted_iota(jnp.int32, (32, 512), 0)
    spread = lax.dot_general(
        mask[...].astype(F32).astype(BF16), at_col.astype(F32).astype(BF16), TN, preferred_element_type=F32
    )
    mask_row = jnp.sum(jnp.where(at_row, spread, 0.0), axis=0, keepdims=True)

    def project(weight):
        turned_weight = weight[...].astype(F32).T.astype(BF16)
        return lax.dot_general(turned_weight, normed[...], NT, preferred_element_type=F32)

    left = mask_row * jax.nn.sigmoid(project(w_a_gate)) * project(w_a_proj)
    right = mask_row * jax.nn.sigmoid(project(w_b_gate)) * project(w_b_proj)
    for part in range(4):
        lanes = slice(part * 128, part * 128 + 128)
        both = jnp.concatenate([left[:, lanes].reshape(16, 8, 128), right[:, lanes].reshape(16, 8, 128)], axis=1)
        z_send[:, part * 16 : part * 16 + 16, :] = both.astype(BF16)

    pl.semaphore_wait(barrier, len(peers))

    z_copies = []
    for n, d in enumerate(FAR_FIRST):
        copy = pltpu.make_async_remote_copy(
            src_ref=z_send.at[(z + d) % NZ], dst_ref=z_recv.at[d], send_sem=z_ss.at[d], recv_sem=z_rs.at[d],
            device_id=z_peers[n], device_id_type=MESH,
        )
        copy.start()
        z_copies.append(copy)
    own = pltpu.make_async_copy(z_send.at[z], z_recv.at[0], local_sem.at[0])
    own.start()

    gate[...] = jax.nn.sigmoid(jnp.dot(normed[...], w_gate[...], preferred_element_type=F32))

    own.wait()
    for copy in z_copies:
        copy.wait_recv()

    for half in range(2):
        blocks = swap_blocks([z_recv[half * 8 + a].astype(F32) for a in range(8)])
        for low in range(8):
            turned[half, low * 64 : low * 64 + 64, :] = blocks[low]
    for side in range(2):
        for channel in range(8):
            halves = []
            for half in range(2):
                rows = [turned[half, pl.ds(part * 16 + side * 8 + channel, 8, stride=64), :] for part in range(4)]
                halves.append(jnp.concatenate(rows, axis=0))
            edges[channel // 4, side, channel % 4] = jnp.concatenate(halves, axis=1).astype(BF16)

    swap = pltpu.make_async_remote_copy(
        src_ref=edges.at[1 - core], dst_ref=shared.at[:, :, pl.ds(pl.multiple_of(core * 32, 32), 32), :],
        send_sem=core_ss, recv_sem=core_rs, device_id=other_core, device_id_type=MESH,
    )
    swap.start()
    keep = pltpu.make_async_copy(
        edges.at[core], shared.at[:, :, pl.ds(pl.multiple_of(core * 32, 32), 32), :], local_sem.at[1]
    )
    keep.start()
    keep.wait()
    swap.wait_recv()

    right_copies, left_copies = [], []
    right_rows = pl.ds(pl.multiple_of((y * 2 + x // 2) * 64, 64), 64)
    left_rows = pl.ds(pl.multiple_of((x // 2) * 64, 64), 64)
    for n, (dy, dx) in enumerate(PLANE):
        copy = pltpu.make_async_remote_copy(
            src_ref=shared.at[1, (x + dx) % NX], dst_ref=right_all.at[x % 2, right_rows, :],
            send_sem=right_ss.at[n], recv_sem=right_rs.at[n], device_id=plane_peers[n], device_id_type=MESH,
        )
        copy.start()
        right_copies.append(copy)
    for n, dx in enumerate(ALONG_X):
        copy = pltpu.make_async_remote_copy(
            src_ref=shared.at[0, (x + dx) % NX], dst_ref=left_all.at[x % 2, left_rows, :],
            send_sem=left_ss.at[n], recv_sem=left_rs.at[n], device_id=device(y, (x + dx) % NX, core, z),
            device_id_type=MESH,
        )
        copy.start()
        left_copies.append(copy)
    own_right = pltpu.make_async_copy(shared.at[1, x], right_all.at[x % 2, right_rows, :], local_sem.at[2])
    own_left = pltpu.make_async_copy(shared.at[0, x], left_all.at[x % 2, left_rows, :], local_sem.at[3])
    own_right.start()
    own_left.start()
    own_right.wait()
    own_left.wait()
    for n, dx in enumerate(ALONG_X):
        source = (x + NX - dx) % NX
        rows = pl.ds(pl.multiple_of((source // 2) * 64, 64), 64)
        pltpu.make_async_remote_copy(
            src_ref=shared.at[0, 0], dst_ref=left_all.at[source % 2, rows, :],
            send_sem=left_ss.at[n], recv_sem=left_rs.at[n], device_id=other_core, device_id_type=MESH,
        ).wait_recv()
    for n, (dy, dx) in enumerate(PLANE):
        source_y, source_x = (y + NY - dy) % NY, (x + NX - dx) % NX
        rows = pl.ds(pl.multiple_of((source_y * 2 + source_x // 2) * 64, 64), 64)
        pltpu.make_async_remote_copy(
            src_ref=shared.at[1, 0], dst_ref=right_all.at[source_x % 2, rows, :],
            send_sem=right_ss.at[n], recv_sem=right_rs.at[n], device_id=other_core, device_id_type=MESH,
        ).wait_recv()

    for half in range(2):
        total = lax.dot_general(
            left_all[0], right_all[0, half * 256 : half * 256 + 256, :], NT, preferred_element_type=F32
        ) + lax.dot_general(
            left_all[1], right_all[1, half * 256 : half * 256 + 256, :], NT, preferred_element_type=F32
        )
        product[half] = total.astype(BF16)

    x_copies = []
    slot = core * 4 + x
    for n, (dx, dc) in enumerate([(dx, dc) for dx in ALONG_X + (0,) for dc in (1, 0) if dx or dc]):
        to_x = (x + dx) % NX
        to_core = (core + dc) % 2
        rows = pl.ds(pl.multiple_of(((to_x // 2) * 2 + to_core) * 32, 32), 32)
        copy = pltpu.make_async_remote_copy(
            src_ref=product.at[to_x % 2, rows, :], dst_ref=product_x.at[slot],
            send_sem=x_ss.at[n], recv_sem=x_rs.at[n], device_id=device(y, to_x, to_core, z), device_id_type=MESH,
        )
        copy.start()
        x_copies.append((copy, dx, dc))
    rows = pl.ds(pl.multiple_of(((x // 2) * 2 + core) * 32, 32), 32)
    own_product = pltpu.make_async_copy(product.at[x % 2, rows, :], product_x.at[slot], local_sem.at[4])
    own_product.start()
    own_product.wait()
    for n, (copy, dx, dc) in enumerate(x_copies):
        source = ((core + dc) % 2) * 4 + (x + NX - dx) % NX
        pltpu.make_async_remote_copy(
            src_ref=product.at[0, pl.ds(0, 32), :], dst_ref=product_x.at[source],
            send_sem=x_ss.at[n], recv_sem=x_rs.at[n], device_id=other_core, device_id_type=MESH,
        ).wait_recv()

    for half in range(2):
        for channel in range(8):
            turned_back[half, channel * 32 : channel * 32 + 32, :] = product_x[
                channel, :, half * 128 : half * 128 + 128
            ].astype(F32)
    for half in range(2):
        rows = []
        for low in range(8):
            rows.append(
                jnp.concatenate(
                    [turned_back[half, pl.ds(part * 8 + low, 8, stride=32), :] for part in range(4)], axis=0
                )
            )
        for low, block in enumerate(swap_blocks(rows)):
            back_send[half * 8 + low] = block.astype(BF16)

    back_copies = []
    for n, d in enumerate(FAR_FIRST):
        copy = pltpu.make_async_remote_copy(
            src_ref=back_send.at[(z + d) % NZ], dst_ref=back_recv.at[z], send_sem=back_ss.at[d], recv_sem=back_rs.at[d],
            device_id=z_peers[n], device_id_type=MESH,
        )
        copy.start()
        back_copies.append(copy)
    own_back = pltpu.make_async_copy(back_send.at[z], back_recv.at[z], local_sem.at[5])
    own_back.start()
    own_back.wait()
    for n, d in enumerate(FAR_FIRST):
        pltpu.make_async_remote_copy(
            src_ref=back_send.at[0], dst_ref=back_recv.at[(z + NZ - d) % NZ], send_sem=back_ss.at[d],
            recv_sem=back_rs.at[d], device_id=other_core, device_id_type=MESH,
        ).wait_recv()

    gain_col = jnp.broadcast_to(out_gain[...], (8, 128)).T[:, :1]
    bias_col = jnp.broadcast_to(out_bias[...], (8, 128)).T[:, :1]
    gathered = back_recv[...].astype(F32)
    for part in range(4):
        contracted = gathered[:, part * 8 : part * 8 + 8, :].reshape(128, 128)
        centred = contracted - jnp.mean(contracted, axis=0, keepdims=True)
        variance = jnp.mean(centred * centred, axis=0, keepdims=True)
        normed_out = (centred * lax.rsqrt(variance + 1e-05) * gain_col + bias_col).T.astype(BF16)
        result = gate[part * 128 : part * 128 + 128, :] * jnp.dot(normed_out, w_out[...], preferred_element_type=F32)
        out_ref[part * 8 : part * 8 + 8] = result.astype(BF16).reshape(8, 16, 128)

    for copy in z_copies + [swap] + right_copies + left_copies + [c for c, _, _ in x_copies] + back_copies:
        copy.wait_send()


def per_device(
    pair, pair_mask, norm_gain, norm_bias, w_a_gate, w_a_proj, w_b_gate, w_b_proj, w_gate, out_gain, out_bias, w_out
):
    args = (
        pair, pair_mask.T, norm_gain.reshape(1, 128), norm_bias.reshape(1, 128), w_a_gate, w_a_proj, w_b_gate, w_b_proj,
        w_gate, out_gain.reshape(1, 128), out_bias.reshape(1, 128), w_out,
    )
    dma = pltpu.SemaphoreType.DMA
    return pl.pallas_call(
        kernel,
        out_shape=jax.ShapeDtypeStruct(pair.shape, BF16),
        in_specs=[pl.BlockSpec(memory_space=pl.ANY)] * len(args),
        out_specs=pl.BlockSpec(memory_space=pltpu.VMEM),
        scratch_shapes=[pltpu.VMEM(a.shape, a.dtype) for a in args]
        + [
            pltpu.VMEM((512, 128), BF16),
            pltpu.VMEM((512, 128), F32),
            pltpu.VMEM((16, 64, 128), BF16),
            pltpu.VMEM((16, 64, 128), BF16),
            pltpu.VMEM((2, 512, 128), F32),
            pltpu.VMEM((2, 2, 4, 32, 256), BF16),
            pltpu.VMEM((2, 4, 64, 256), BF16),
            pltpu.VMEM((2, 128, 256), BF16),
            pltpu.VMEM((2, 512, 256), BF16),
            pltpu.VMEM((2, 128, 256), BF16),
            pltpu.VMEM((8, 32, 256), BF16),
            pltpu.VMEM((2, 256, 128), F32),
            pltpu.VMEM((16, 32, 128), BF16),
            pltpu.VMEM((16, 32, 128), BF16),
            dma((12,)), dma((16,)), dma((16,)), dma(()), dma(()), dma((15,)), dma((15,)), dma((3,)), dma((3,)),
            dma((7,)), dma((7,)), dma((16,)), dma((16,)), dma((6,)),
        ],
        compiler_params=pltpu.CompilerParams(collective_id=0, has_side_effects=True, vmem_limit_bytes=60 << 20),
        name="triangle",
    )(*args)


def solution(mesh):
    return jax.shard_map(
        per_device,
        mesh=mesh,
        in_specs=(P("row", "col", None), P("row", "col")) + (P(),) * 10,
        out_specs=P("row", "col", None),
        check_vma=False,
    )
```

```python
import jax
import jax.numpy as jnp
from jax import lax
from jax.experimental import pallas as pl
from jax.experimental.pallas import tpu as pltpu
from jax.sharding import PartitionSpec as P

MESH = pl.DeviceIdType.MESH
F32, BF16 = jnp.float32, jnp.bfloat16
NZ, NX, NY = 16, 4, 4
FAR_FIRST = (8, 7, 9, 6, 10, 5, 11, 4, 12, 3, 13, 2, 14, 1, 15)
PLANE = tuple((dy, dx) for dy in (2, 1, 3, 0) for dx in (2, 1, 3, 0) if dy or dx)
ALONG_X = (2, 1, 3)
X_AND_CORE = tuple((dx, dc) for dx in ALONG_X + (0,) for dc in (1, 0) if dx or dc)
NT = (((1,), (1,)), ((), ()))
TN = (((0,), (0,)), ((), ()))


def swap_blocks(arrays):
    arrays = list(arrays)
    lane = lax.broadcasted_iota(jnp.int32, arrays[0].shape, 1)
    for bit in range(3):
        step = 1 << bit
        upper = ((lane // 16) // step) % 2 == 1
        for a in range(8):
            if not a & step:
                low, high = arrays[a], arrays[a | step]
                arrays[a] = jnp.where(upper, pltpu.roll(high, 16 * step, 1), low)
                arrays[a | step] = jnp.where(upper, high, pltpu.roll(low, 128 - 16 * step, 1))
    return arrays


def kernel(
    pair_hbm, mask_hbm, norm_gain_hbm, norm_bias_hbm, w_a_gate_hbm, w_a_proj_hbm, w_b_gate_hbm, w_b_proj_hbm,
    w_gate_hbm, out_gain_hbm, out_bias_hbm, w_out_hbm,
    out_ref,
    pair, mask, norm_gain, norm_bias, w_a_gate, w_a_proj, w_b_gate, w_b_proj, w_gate, out_gain, out_bias, w_out,
    normed, gate, z_send, z_recv, turned, left_edges, right_edges, shared, left_all, right_all, product, product_x,
    turned_back, back_send, back_recv,
    in_sem, z_ss, z_rs, core_ss, core_rs, right_ss, right_rs, left_ss, left_rs, x_ss, x_rs, back_ss, back_rs, local_sem,
):
    row, col = lax.axis_index("row"), lax.axis_index("col")
    y, core = row // 4, row % 2
    x = ((row // 2) % 2) * 2 + col // 16
    z = col % 16

    def device(y, x, core, z):
        return {"row": y * 4 + (x // 2) * 2 + core, "col": (x % 2) * 16 + z}

    def remote(src, dst, ss, rs, to):
        return pltpu.make_async_remote_copy(
            src_ref=src, dst_ref=dst, send_sem=ss, recv_sem=rs, device_id=to, device_id_type=MESH
        )

    z_peers = [device(y, x, core, (z + d) % NZ) for d in FAR_FIRST]
    plane_peers = [device((y + dy) % NY, (x + dx) % NX, core, z) for dy, dx in PLANE]
    other_core = device(y, x, 1 - core, z)
    x_other_core = [device(y, (x + dx) % NX, 1 - core, z) for dx in ALONG_X]
    barrier = pltpu.get_barrier_semaphore()
    peers = z_peers + plane_peers + [other_core] + x_other_core
    for peer in peers:
        pl.semaphore_signal(barrier, inc=1, device_id=peer, device_id_type=MESH)

    loads = [
        pltpu.make_async_copy(src, dst, in_sem.at[n])
        for n, (src, dst) in enumerate(
            (
                (pair_hbm, pair), (norm_gain_hbm, norm_gain), (norm_bias_hbm, norm_bias), (w_b_gate_hbm, w_b_gate),
                (w_b_proj_hbm, w_b_proj), (mask_hbm, mask), (w_a_gate_hbm, w_a_gate), (w_a_proj_hbm, w_a_proj),
                (w_gate_hbm, w_gate), (out_gain_hbm, out_gain), (out_bias_hbm, out_bias), (w_out_hbm, w_out),
            )
        )
    ]
    for load in loads:
        load.start()
    for load in loads[:6]:
        load.wait()

    values = pair[...].astype(F32).reshape(512, 128)
    centred = values - jnp.mean(values, axis=1, keepdims=True)
    variance = jnp.mean(centred * centred, axis=1, keepdims=True)
    normed[...] = (centred * lax.rsqrt(variance + 1e-05) * norm_gain[...] + norm_bias[...]).astype(BF16)

    at_col = lax.broadcasted_iota(jnp.int32, (16, 512), 1) % 16 == lax.broadcasted_iota(jnp.int32, (16, 512), 0)
    at_row = lax.broadcasted_iota(jnp.int32, (32, 512), 1) // 16 == lax.broadcasted_iota(jnp.int32, (32, 512), 0)
    spread = lax.dot_general(
        mask[...].astype(F32).astype(BF16), at_col.astype(F32).astype(BF16), TN, preferred_element_type=F32
    )
    mask_row = jnp.sum(jnp.where(at_row, spread, 0.0), axis=0, keepdims=True)

    def project(weight):
        turned_weight = weight[...].astype(F32).T.astype(BF16)
        return lax.dot_general(turned_weight, normed[...], NT, preferred_element_type=F32)

    def edges_of(side, w_gate, w_proj):
        edges = mask_row * jax.nn.sigmoid(project(w_gate)) * project(w_proj)
        parts = [edges[:, part * 128 : part * 128 + 128].reshape(16, 8, 128) for part in range(4)]
        z_send[side] = jnp.concatenate(parts, axis=1).astype(BF16)

    def start_along_z(side):
        copies = [
            remote(z_send.at[side, (z + d) % NZ], z_recv.at[side, d], z_ss.at[side, d], z_rs.at[side, d], z_peers[n])
            for n, d in enumerate(FAR_FIRST)
        ]
        for copy in copies:
            copy.start()
        own = pltpu.make_async_copy(z_send.at[side, z], z_recv.at[side, 0], local_sem.at[side])
        own.start()
        return own, copies

    def finish_along_z(side, own, copies):
        own.wait()
        for copy in copies:
            copy.wait_recv()
        for half in range(2):
            blocks = swap_blocks([z_recv[side, half * 8 + a].astype(F32) for a in range(8)])
            for low in range(8):
                turned[side, half, low * 32 : low * 32 + 32, :] = blocks[low]

    def channel_rows(side, channel):
        halves = []
        for half in range(2):
            rows = [turned[side, half, pl.ds(part * 8 + channel, 8, stride=32), :] for part in range(4)]
            halves.append(jnp.concatenate(rows, axis=0))
        return jnp.concatenate(halves, axis=1).astype(BF16)

    edges_of(1, w_b_gate, w_b_proj)
    pl.semaphore_wait(barrier, len(peers))
    right_own, right_z = start_along_z(1)
    for load in loads[6:]:
        load.wait()
    edges_of(0, w_a_gate, w_a_proj)
    left_own, left_z = start_along_z(0)
    gate[...] = jax.nn.sigmoid(jnp.dot(normed[...], w_gate[...], preferred_element_type=F32))

    finish_along_z(1, right_own, right_z)
    for channel in range(8):
        right_edges[channel // 4, channel % 4] = channel_rows(1, channel)
    own_rows = pl.ds(pl.multiple_of(core * 32, 32), 32)
    swap = remote(right_edges.at[1 - core], shared.at[:, own_rows, :], core_ss, core_rs, other_core)
    swap.start()
    keep = pltpu.make_async_copy(right_edges.at[core], shared.at[:, own_rows, :], local_sem.at[2])
    keep.start()
    keep.wait()
    swap.wait_recv()

    def right_rows(y, x):
        return right_all.at[x % 2, pl.ds(pl.multiple_of((y * 2 + x // 2) * 64, 64), 64), :]

    right_copies = [
        remote(shared.at[(x + dx) % NX], right_rows(y, x), right_ss.at[n], right_rs.at[n], plane_peers[n])
        for n, (dy, dx) in enumerate(PLANE)
    ]
    for copy in right_copies:
        copy.start()
    own_right = pltpu.make_async_copy(shared.at[x], right_rows(y, x), local_sem.at[3])
    own_right.start()

    finish_along_z(0, left_own, left_z)
    for channel in range(8):
        left_edges[channel] = channel_rows(0, channel)

    def left_rows(x, core):
        return left_all.at[x % 2, pl.ds(pl.multiple_of(((x // 2) * 2 + core) * 32, 32), 32), :]

    left_copies = []
    for n, (dx, dc) in enumerate(X_AND_CORE):
        to_x, to_core = (x + dx) % NX, (core + dc) % 2
        copy = remote(
            left_edges.at[to_core * 4 + to_x], left_rows(x, core), left_ss.at[n], left_rs.at[n],
            device(y, to_x, to_core, z),
        )
        copy.start()
        left_copies.append(copy)
    own_left = pltpu.make_async_copy(left_edges.at[core * 4 + x], left_rows(x, core), local_sem.at[4])
    own_left.start()
    own_right.wait()
    own_left.wait()
    for n, (dy, dx) in enumerate(PLANE):
        arrived = right_rows((y + NY - dy) % NY, (x + NX - dx) % NX)
        remote(shared.at[0], arrived, right_ss.at[n], right_rs.at[n], other_core).wait_recv()
    for n, (dx, dc) in enumerate(X_AND_CORE):
        arrived = left_rows((x + NX - dx) % NX, (core + dc) % 2)
        remote(left_edges.at[0], arrived, left_ss.at[n], left_rs.at[n], other_core).wait_recv()

    for half in range(2):
        total = lax.dot_general(
            left_all[0], right_all[0, half * 256 : half * 256 + 256, :], NT, preferred_element_type=F32
        ) + lax.dot_general(
            left_all[1], right_all[1, half * 256 : half * 256 + 256, :], NT, preferred_element_type=F32
        )
        product[half] = total.astype(BF16)

    def product_rows(x, core):
        return product.at[x % 2, pl.ds(pl.multiple_of(((x // 2) * 2 + core) * 32, 32), 32), :]

    x_copies = []
    for n, (dx, dc) in enumerate(X_AND_CORE):
        to_x, to_core = (x + dx) % NX, (core + dc) % 2
        copy = remote(
            product_rows(to_x, to_core), product_x.at[core * 4 + x], x_ss.at[n], x_rs.at[n], device(y, to_x, to_core, z)
        )
        copy.start()
        x_copies.append(copy)
    own_product = pltpu.make_async_copy(product_rows(x, core), product_x.at[core * 4 + x], local_sem.at[5])
    own_product.start()
    own_product.wait()
    for n, (dx, dc) in enumerate(X_AND_CORE):
        arrived = product_x.at[((core + dc) % 2) * 4 + (x + NX - dx) % NX]
        remote(product_rows(0, 0), arrived, x_ss.at[n], x_rs.at[n], other_core).wait_recv()

    for half in range(2):
        for channel in range(8):
            turned_back[half, channel * 32 : channel * 32 + 32, :] = product_x[
                channel, :, half * 128 : half * 128 + 128
            ].astype(F32)
    for half in range(2):
        rows = []
        for low in range(8):
            rows.append(
                jnp.concatenate(
                    [turned_back[half, pl.ds(part * 8 + low, 8, stride=32), :] for part in range(4)], axis=0
                )
            )
        for low, block in enumerate(swap_blocks(rows)):
            back_send[half * 8 + low] = block.astype(BF16)

    back_copies = [
        remote(back_send.at[(z + d) % NZ], back_recv.at[z], back_ss.at[d], back_rs.at[d], z_peers[n])
        for n, d in enumerate(FAR_FIRST)
    ]
    for copy in back_copies:
        copy.start()
    own_back = pltpu.make_async_copy(back_send.at[z], back_recv.at[z], local_sem.at[6])
    own_back.start()
    own_back.wait()
    for d in FAR_FIRST:
        arrived = back_recv.at[(z + NZ - d) % NZ]
        remote(back_send.at[0], arrived, back_ss.at[d], back_rs.at[d], other_core).wait_recv()

    gain_col = jnp.broadcast_to(out_gain[...], (8, 128)).T[:, :1]
    bias_col = jnp.broadcast_to(out_bias[...], (8, 128)).T[:, :1]
    gathered = back_recv[...].astype(F32)
    for part in range(4):
        contracted = gathered[:, part * 8 : part * 8 + 8, :].reshape(128, 128)
        centred = contracted - jnp.mean(contracted, axis=0, keepdims=True)
        variance = jnp.mean(centred * centred, axis=0, keepdims=True)
        normed_out = (centred * lax.rsqrt(variance + 1e-05) * gain_col + bias_col).T.astype(BF16)
        result = gate[part * 128 : part * 128 + 128, :] * jnp.dot(normed_out, w_out[...], preferred_element_type=F32)
        out_ref[part * 8 : part * 8 + 8] = result.astype(BF16).reshape(8, 16, 128)

    for copy in right_z + left_z + [swap] + right_copies + left_copies + x_copies + back_copies:
        copy.wait_send()


def per_device(
    pair, pair_mask, norm_gain, norm_bias, w_a_gate, w_a_proj, w_b_gate, w_b_proj, w_gate, out_gain, out_bias, w_out
):
    args = (
        pair, pair_mask.T, norm_gain.reshape(1, 128), norm_bias.reshape(1, 128), w_a_gate, w_a_proj, w_b_gate, w_b_proj,
        w_gate, out_gain.reshape(1, 128), out_bias.reshape(1, 128), w_out,
    )
    dma = pltpu.SemaphoreType.DMA
    return pl.pallas_call(
        kernel,
        out_shape=pltpu.VMEM(pair.shape, BF16),
        in_specs=[pl.BlockSpec(memory_space=pl.ANY)] * len(args),
        out_specs=pl.BlockSpec(memory_space=pltpu.VMEM),
        scratch_shapes=[pltpu.VMEM(a.shape, a.dtype) for a in args]
        + [
            pltpu.VMEM((512, 128), BF16),
            pltpu.VMEM((512, 128), F32),
            pltpu.VMEM((2, 16, 32, 128), BF16),
            pltpu.VMEM((2, 16, 32, 128), BF16),
            pltpu.VMEM((2, 2, 256, 128), F32),
            pltpu.VMEM((8, 32, 256), BF16),
            pltpu.VMEM((2, 4, 32, 256), BF16),
            pltpu.VMEM((4, 64, 256), BF16),
            pltpu.VMEM((2, 128, 256), BF16),
            pltpu.VMEM((2, 512, 256), BF16),
            pltpu.VMEM((2, 128, 256), BF16),
            pltpu.VMEM((8, 32, 256), BF16),
            pltpu.VMEM((2, 256, 128), F32),
            pltpu.VMEM((16, 32, 128), BF16),
            pltpu.VMEM((16, 32, 128), BF16),
            dma((12,)), dma((2, 16)), dma((2, 16)), dma(()), dma(()), dma((15,)), dma((15,)), dma((7,)), dma((7,)),
            dma((7,)), dma((7,)), dma((16,)), dma((16,)), dma((7,)),
        ],
        compiler_params=pltpu.CompilerParams(collective_id=0, has_side_effects=True, vmem_limit_bytes=32 << 20),
        name="triangle",
    )(*[pltpu.with_memory_space_constraint(a, pltpu.HBM) for a in args])


def solution(mesh):
    return jax.shard_map(
        per_device,
        mesh=mesh,
        in_specs=(P("row", "col", None), P("row", "col")) + (P(),) * 10,
        out_specs=P("row", "col", None),
        check_vma=False,
    )
```

```python
import jax
import jax.numpy as jnp
from jax import lax
from jax.experimental import pallas as pl
from jax.experimental.pallas import tpu as pltpu
from jax.sharding import PartitionSpec as P

MESH = pl.DeviceIdType.MESH
F32, BF16 = jnp.float32, jnp.bfloat16
NZ, NX, NY = 16, 4, 4
FAR_FIRST = (8, 7, 9, 6, 10, 5, 11, 4, 12, 3, 13, 2, 14, 1, 15)
NEAR = (4, 12, 3, 13, 2, 14, 1, 15)
ALONG_Y = (2, 1, 3)
X_AND_CORE = tuple((dx, dc) for dx in (2, 1, 3, 0) for dc in (1, 0) if dx or dc)
NT = (((1,), (1,)), ((), ()))
TN = (((0,), (0,)), ((), ()))


def swap_blocks(arrays):
    arrays = list(arrays)
    lane = lax.broadcasted_iota(jnp.int32, arrays[0].shape, 1)
    for bit in range(3):
        step = 1 << bit
        upper = ((lane // 16) // step) % 2 == 1
        for a in range(8):
            if not a & step:
                low, high = arrays[a], arrays[a | step]
                arrays[a] = jnp.where(upper, pltpu.roll(high, 16 * step, 1), low)
                arrays[a | step] = jnp.where(upper, high, pltpu.roll(low, 128 - 16 * step, 1))
    return arrays


def kernel(
    pair_hbm, mask_hbm, norm_gain_hbm, norm_bias_hbm, w_a_gate_hbm, w_a_proj_hbm, w_b_gate_hbm, w_b_proj_hbm,
    w_gate_hbm, out_gain_hbm, out_bias_hbm, w_out_hbm,
    out_ref,
    pair, mask, norm_gain, norm_bias, w_a_gate, w_a_proj, w_b_gate, w_b_proj, w_gate, out_gain, out_bias, w_out,
    normed, gate, x_send, x_recv, x_rows, z_send, z_recv, turned, left, right_all, product, back_z_send, back_z_recv,
    back_rows, back_x_send, back_x_recv,
    in_sem, x_ss, x_rs, z_ss, z_rs, y_ss, y_rs, back_z_ss, back_z_rs, back_x_ss, back_x_rs, ring_sem,
):
    row, col = lax.axis_index("row"), lax.axis_index("col")
    y, core = row // 4, row % 2
    x = ((row // 2) % 2) * 2 + col // 16
    z = col % 16

    def device(y, x, core, z):
        return {"row": y * 4 + (x // 2) * 2 + core, "col": (x % 2) * 16 + z}

    def remote(src, dst, ss, rs, to):
        return pltpu.make_async_remote_copy(
            src_ref=src, dst_ref=dst, send_sem=ss, recv_sem=rs, device_id=to, device_id_type=MESH
        )

    slot = core * 4 + x
    other_core = device(y, x, 1 - core, z)
    z_peers = [device(y, x, core, (z + d) % NZ) for d in FAR_FIRST]
    x_peers = [device(y, (x + dx) % NX, (core + dc) % 2, z) for dx, dc in X_AND_CORE]
    y_peers = [device((y + d) % NY, x, core, z) for d in ALONG_Y]
    barrier = pltpu.get_barrier_semaphore()
    peers = [device(y, x, core, (z + d) % NZ) for d in NEAR] + x_peers + y_peers
    for peer in peers:
        pl.semaphore_signal(barrier, inc=1, device_id=peer, device_id_type=MESH)

    loads = [
        pltpu.make_async_copy(src, dst, in_sem.at[n])
        for n, (src, dst) in enumerate(
            (
                (pair_hbm, pair), (norm_gain_hbm, norm_gain), (norm_bias_hbm, norm_bias), (w_b_gate_hbm, w_b_gate),
                (w_b_proj_hbm, w_b_proj), (mask_hbm, mask), (w_a_gate_hbm, w_a_gate), (w_a_proj_hbm, w_a_proj),
                (w_gate_hbm, w_gate), (out_gain_hbm, out_gain), (out_bias_hbm, out_bias), (w_out_hbm, w_out),
            )
        )
    ]
    for load in loads:
        load.start()
    for load in loads[:6]:
        load.wait()

    values = pair[...].astype(F32).reshape(512, 128)
    centred = values - jnp.mean(values, axis=1, keepdims=True)
    variance = jnp.mean(centred * centred, axis=1, keepdims=True)
    normed[...] = (centred * lax.rsqrt(variance + 1e-05) * norm_gain[...] + norm_bias[...]).astype(BF16)

    at_col = lax.broadcasted_iota(jnp.int32, (16, 512), 1) % 16 == lax.broadcasted_iota(jnp.int32, (16, 512), 0)
    at_row = lax.broadcasted_iota(jnp.int32, (32, 512), 1) // 16 == lax.broadcasted_iota(jnp.int32, (32, 512), 0)
    spread = lax.dot_general(
        mask[...].astype(F32).astype(BF16), at_col.astype(F32).astype(BF16), TN, preferred_element_type=F32
    )
    mask_row = jnp.sum(jnp.where(at_row, spread, 0.0), axis=0, keepdims=True)

    def project(weight):
        turned_weight = weight[...].astype(F32).T.astype(BF16)
        return lax.dot_general(turned_weight, normed[...], NT, preferred_element_type=F32)

    def edges_of(side, w_gate, w_proj):
        edges = mask_row * jax.nn.sigmoid(project(w_gate)) * project(w_proj)
        x_send[side] = edges.reshape(8, 16, 512).astype(BF16)

    def slot_at(dx, dc):
        return ((core + dc) % 2) * 4 + (x + dx + NX) % NX

    def start_along_x(side):
        copies = [
            remote(x_send.at[side, slot_at(dx, dc)], x_recv.at[side, slot], x_ss.at[side, n], x_rs.at[side, n], x_peers[n])
            for n, (dx, dc) in enumerate(X_AND_CORE)
        ]
        for copy in copies:
            copy.start()
        x_recv[side, slot] = x_send[side, slot]
        return copies

    def start_along_z(side):
        for n, (dx, dc) in enumerate(X_AND_CORE):
            arrived = x_recv.at[side, slot_at(-dx, dc)]
            remote(x_send.at[side, 0], arrived, x_ss.at[side, n], x_rs.at[side, n], x_peers[n]).wait_recv()
        for part in range(4):
            lanes = slice(part * 128, part * 128 + 128)
            x_rows[side, part] = x_recv[side, :, :, lanes].astype(F32).reshape(128, 128)
        for plane in range(NZ):
            rows = [x_rows[side, part, pl.ds(plane, 8, stride=16), :] for part in range(4)]
            z_send[side, plane] = jnp.concatenate(rows, axis=0).astype(BF16)
        copies = [
            remote(z_send.at[side, (z + d) % NZ], z_recv.at[side, d], z_ss.at[side, d], z_rs.at[side, d], z_peers[n])
            for n, d in enumerate(FAR_FIRST)
        ]
        for copy in copies:
            copy.start()
        z_recv[side, 0] = z_send[side, z]
        return copies

    def finish_along_z(side, copies):
        for copy in copies:
            copy.wait_recv()
        for half in range(2):
            blocks = swap_blocks([z_recv[side, half * 8 + a].astype(F32) for a in range(8)])
            for low in range(8):
                turned[side, half, low * 32 : low * 32 + 32, :] = blocks[low]
        result = []
        for x_low in range(2):
            halves = []
            for half in range(2):
                starts = [
                    part * 8 + of_core * 4 + x_high * 2 + x_low
                    for x_high in range(2) for of_core in range(2) for part in range(4)
                ]
                rows = [turned[side, half, pl.ds(start, 8, stride=32), :] for start in starts]
                halves.append(jnp.concatenate(rows, axis=0))
            result.append(jnp.concatenate(halves, axis=1).astype(BF16))
        return result

    edges_of(1, w_b_gate, w_b_proj)
    pl.semaphore_wait(barrier, len(peers))
    for d in (4, 12):
        pl.semaphore_signal(ring_sem, inc=1, device_id=device(y, x, core, (z + d) % NZ), device_id_type=MESH)
    right_x = start_along_x(1)
    for load in loads[6:]:
        load.wait()
    edges_of(0, w_a_gate, w_a_proj)
    left_x = start_along_x(0)
    pl.semaphore_wait(ring_sem, 2)
    right_z = start_along_z(1)
    left_z = start_along_z(0)
    gate[...] = jax.nn.sigmoid(jnp.dot(normed[...], w_gate[...], preferred_element_type=F32))

    for x_low, rows in enumerate(finish_along_z(1, right_z)):
        right_all[y, x_low] = rows
    y_copies = [
        remote(right_all.at[y], right_all.at[y], y_ss.at[d], y_rs.at[d], y_peers[n]) for n, d in enumerate(ALONG_Y)
    ]
    for copy in y_copies:
        copy.start()
    for x_low, rows in enumerate(finish_along_z(0, left_z)):
        left[x_low] = rows

    def contract(of_y):
        d = (y + NY - of_y) % NY

        @pl.when(d != 0)
        def _():
            remote(right_all.at[y], right_all.at[of_y], y_ss.at[d], y_rs.at[d], other_core).wait_recv()

        product[of_y] = lax.dot_general(left[0], right_all[of_y, 0], NT, preferred_element_type=F32) + lax.dot_general(
            left[1], right_all[of_y, 1], NT, preferred_element_type=F32
        )
        blocks = swap_blocks([product[of_y, pl.ds(low, 16, stride=8), :] for low in range(8)])
        for low in range(8):
            back_z_send[(of_y % 2) * 8 + low, of_y // 2] = blocks[low].astype(BF16)

    def back_z_copy(to_z):
        return remote(
            back_z_send.at[to_z], back_z_recv.at[z], back_z_ss.at[to_z], back_z_rs.at[z], device(y, x, core, to_z)
        )

    for odd in range(2):
        contract((y // 2) * 2 + odd)
        contract((1 - y // 2) * 2 + odd)
        for to_z in range(odd * 8, odd * 8 + 8):

            @pl.when(z != to_z)
            def _():
                back_z_copy(to_z).start()

    back_z_recv[z] = back_z_send[z]
    for d in FAR_FIRST:
        from_z = (z + NZ - d) % NZ
        remote(
            back_z_send.at[0], back_z_recv.at[from_z], back_z_ss.at[from_z], back_z_rs.at[from_z], other_core
        ).wait_recv()

    back_rows[...] = back_z_recv[...].astype(F32).reshape(512, 128)
    for to_core in range(2):
        for to_x in range(NX):
            start = (to_x % 2) * 16 + (to_x // 2) * 8 + to_core * 4
            rows = [back_rows[pl.ds(start + part, 16, stride=32), :] for part in range(4)]
            back_x_send[to_core * 4 + to_x] = jnp.concatenate(rows, axis=0).astype(BF16)
    back_x = [
        remote(back_x_send.at[slot_at(dx, dc)], back_x_recv.at[slot], back_x_ss.at[n], back_x_rs.at[n], x_peers[n])
        for n, (dx, dc) in enumerate(X_AND_CORE)
    ]
    for copy in back_x:
        copy.start()
    back_x_recv[slot] = back_x_send[slot]
    for n, (dx, dc) in enumerate(X_AND_CORE):
        arrived = back_x_recv.at[slot_at(-dx, dc)]
        remote(back_x_send.at[0], arrived, back_x_ss.at[n], back_x_rs.at[n], x_peers[n]).wait_recv()

    gain_col = jnp.broadcast_to(out_gain[...], (8, 128)).T[:, :1]
    bias_col = jnp.broadcast_to(out_bias[...], (8, 128)).T[:, :1]
    for part in range(4):
        contracted = back_x_recv[:, part * 16 : part * 16 + 16, :].astype(F32).reshape(128, 128)
        centred = contracted - jnp.mean(contracted, axis=0, keepdims=True)
        variance = jnp.mean(centred * centred, axis=0, keepdims=True)
        normed_out = (centred * lax.rsqrt(variance + 1e-05) * gain_col + bias_col).T.astype(BF16)
        result = gate[part * 128 : part * 128 + 128, :] * jnp.dot(normed_out, w_out[...], preferred_element_type=F32)
        out_ref[part * 8 : part * 8 + 8] = result.astype(BF16).reshape(8, 16, 128)

    for copy in right_x + left_x + right_z + left_z + y_copies + back_x:
        copy.wait_send()
    for d in FAR_FIRST:
        back_z_copy((z + d) % NZ).wait_send()


def per_device(
    pair, pair_mask, norm_gain, norm_bias, w_a_gate, w_a_proj, w_b_gate, w_b_proj, w_gate, out_gain, out_bias, w_out
):
    args = (
        pair, pair_mask.T, norm_gain.reshape(1, 128), norm_bias.reshape(1, 128), w_a_gate, w_a_proj, w_b_gate, w_b_proj,
        w_gate, out_gain.reshape(1, 128), out_bias.reshape(1, 128), w_out,
    )
    dma = pltpu.SemaphoreType.DMA
    return pl.pallas_call(
        kernel,
        out_shape=pltpu.VMEM(pair.shape, BF16),
        in_specs=[pl.BlockSpec(memory_space=pl.ANY)] * len(args),
        out_specs=pl.BlockSpec(memory_space=pltpu.VMEM),
        scratch_shapes=[pltpu.VMEM(a.shape, a.dtype) for a in args]
        + [
            pltpu.VMEM((512, 128), BF16),
            pltpu.VMEM((512, 128), F32),
            pltpu.VMEM((2, 8, 16, 512), BF16),
            pltpu.VMEM((2, 8, 16, 512), BF16),
            pltpu.VMEM((2, 4, 128, 128), F32),
            pltpu.VMEM((2, 16, 32, 128), BF16),
            pltpu.VMEM((2, 16, 32, 128), BF16),
            pltpu.VMEM((2, 2, 256, 128), F32),
            pltpu.VMEM((2, 128, 256), BF16),
            pltpu.VMEM((4, 2, 128, 256), BF16),
            pltpu.VMEM((4, 128, 128), F32),
            pltpu.VMEM((16, 2, 16, 128), BF16),
            pltpu.VMEM((16, 2, 16, 128), BF16),
            pltpu.VMEM((512, 128), F32),
            pltpu.VMEM((8, 64, 128), BF16),
            pltpu.VMEM((8, 64, 128), BF16),
            dma((12,)), dma((2, 7)), dma((2, 7)), dma((2, 16)), dma((2, 16)), dma((4,)), dma((4,)), dma((16,)), dma((16,)),
            dma((7,)), dma((7,)), pltpu.SemaphoreType.REGULAR,
        ],
        compiler_params=pltpu.CompilerParams(collective_id=0, has_side_effects=True, vmem_limit_bytes=32 << 20),
        name="triangle",
    )(*[pltpu.with_memory_space_constraint(a, pltpu.HBM) for a in args])


def solution(mesh):
    return jax.shard_map(
        per_device,
        mesh=mesh,
        in_specs=(P("row", "col", None), P("row", "col")) + (P(),) * 10,
        out_specs=P("row", "col", None),
        check_vma=False,
    )
```

```python
import jax
import jax.numpy as jnp
from jax import lax
from jax.experimental import pallas as pl
from jax.experimental.pallas import tpu as pltpu
from jax.sharding import PartitionSpec as P

MESH = pl.DeviceIdType.MESH
F32, BF16 = jnp.float32, jnp.bfloat16
NZ, NX, NY = 16, 4, 4
FAR_FIRST = (8, 7, 9, 6, 10, 5, 11, 4, 12, 3, 13, 2, 14, 1, 15)
NEAR = (4, 12, 3, 13, 2, 14, 1, 15)
ALONG_Y = (2, 1, 3)
X_AND_CORE = tuple((dx, dc) for dx in (2, 1, 3, 0) for dc in (1, 0) if dx or dc)
NT = (((1,), (1,)), ((), ()))
TN = (((0,), (0,)), ((), ()))


def swap_blocks(arrays):
    arrays = list(arrays)
    lane = lax.broadcasted_iota(jnp.int32, arrays[0].shape, 1)
    for bit in range(3):
        step = 1 << bit
        upper = ((lane // 16) // step) % 2 == 1
        for a in range(8):
            if not a & step:
                low, high = arrays[a], arrays[a | step]
                arrays[a] = jnp.where(upper, pltpu.roll(high, 16 * step, 1), low)
                arrays[a | step] = jnp.where(upper, high, pltpu.roll(low, 128 - 16 * step, 1))
    return arrays


def kernel(
    pair_hbm, mask_hbm, norm_gain_hbm, norm_bias_hbm, w_a_gate_hbm, w_a_proj_hbm, w_b_gate_hbm, w_b_proj_hbm,
    w_gate_hbm, out_gain_hbm, out_bias_hbm, w_out_hbm,
    out_ref,
    pair, mask, norm_gain, norm_bias, w_a_gate, w_a_proj, w_b_gate, w_b_proj, w_gate, out_gain, out_bias, w_out,
    normed, gate, x_send, x_recv, left_rows, right_rows, left_send, left_recv, right_send, right_recv, left_turned,
    right_turned, left, right_all, product, back_z_send, back_z_recv, back_rows, back_x_send, back_x_recv,
    in_sem, x_ss, x_rs, left_ss, left_rs, right_ss, right_rs, y_ss, y_rs, back_z_ss, back_z_rs, back_x_ss, back_x_rs,
    ring_sem, core_sem,
):
    row, col = lax.axis_index("row"), lax.axis_index("col")
    y, core = row // 4, row % 2
    x = ((row // 2) % 2) * 2 + col // 16
    z = col % 16

    def device(y, x, core, z):
        return {"row": y * 4 + (x // 2) * 2 + core, "col": (x % 2) * 16 + z}

    def slot_of(x, core):
        return (x // 2) * 4 + core * 2 + x % 2

    def slot_at(dx, dc):
        return slot_of((x + dx + NX) % NX, (core + dc) % 2)

    def remote(src, dst, ss, rs, to):
        return pltpu.make_async_remote_copy(
            src_ref=src, dst_ref=dst, send_sem=ss, recv_sem=rs, device_id=to, device_id_type=MESH
        )

    slot = slot_of(x, core)
    other_core = device(y, x, 1 - core, z)
    x_peers = [device(y, (x + dx) % NX, (core + dc) % 2, z) for dx, dc in X_AND_CORE]
    y_peers = [device((y + d) % NY, x, core, z) for d in ALONG_Y]
    barrier = pltpu.get_barrier_semaphore()
    peers = [device(y, x, core, (z + d) % NZ) for d in NEAR] + x_peers + y_peers
    for peer in peers:
        pl.semaphore_signal(barrier, inc=1, device_id=peer, device_id_type=MESH)

    loads = [
        pltpu.make_async_copy(src, dst, in_sem.at[n])
        for n, (src, dst) in enumerate(
            (
                (pair_hbm, pair), (norm_gain_hbm, norm_gain), (norm_bias_hbm, norm_bias), (w_b_gate_hbm, w_b_gate),
                (w_b_proj_hbm, w_b_proj), (mask_hbm, mask), (w_a_gate_hbm, w_a_gate), (w_a_proj_hbm, w_a_proj),
                (w_gate_hbm, w_gate), (out_gain_hbm, out_gain), (out_bias_hbm, out_bias), (w_out_hbm, w_out),
            )
        )
    ]
    for load in loads:
        load.start()
    for load in loads[:6]:
        load.wait()

    values = pair[...].astype(F32).reshape(512, 128)
    centred = values - jnp.mean(values, axis=1, keepdims=True)
    variance = jnp.mean(centred * centred, axis=1, keepdims=True)
    normed[...] = (centred * lax.rsqrt(variance + 1e-05) * norm_gain[...] + norm_bias[...]).astype(BF16)

    at_col = lax.broadcasted_iota(jnp.int32, (16, 512), 1) % 16 == lax.broadcasted_iota(jnp.int32, (16, 512), 0)
    at_row = lax.broadcasted_iota(jnp.int32, (32, 512), 1) // 16 == lax.broadcasted_iota(jnp.int32, (32, 512), 0)
    spread = lax.dot_general(
        mask[...].astype(F32).astype(BF16), at_col.astype(F32).astype(BF16), TN, preferred_element_type=F32
    )
    mask_row = jnp.sum(jnp.where(at_row, spread, 0.0), axis=0, keepdims=True)

    def project(weight):
        turned_weight = weight[...].astype(F32).T.astype(BF16)
        return lax.dot_general(turned_weight, normed[...], NT, preferred_element_type=F32)

    def edges_of(side, w_gate, w_proj):
        edges = mask_row * jax.nn.sigmoid(project(w_gate)) * project(w_proj)
        x_send[side] = edges.reshape(8, 16, 512).astype(BF16)

    def start_along_x(side):
        for n, (dx, dc) in enumerate(X_AND_CORE):
            remote(
                x_send.at[side, slot_at(dx, dc)], x_recv.at[side, slot], x_ss.at[side, n], x_rs.at[side, n], x_peers[n]
            ).start()
        x_recv[side, slot] = x_send[side, slot]

    def wait_along_x(side, first_slot, slots):
        for n, (dx, dc) in enumerate(X_AND_CORE):
            source = slot_at(-dx, dc)

            def wait():
                remote(
                    x_send.at[side, 0], x_recv.at[side, source], x_ss.at[side, n], x_rs.at[side, n], other_core
                ).wait_recv()

            if slots == 8:
                wait()
            else:
                pl.when(source // 4 == first_slot // 4)(wait)

    def start_along_z(send, recv, ss, rs):
        for d in FAR_FIRST:
            remote(send.at[(z + d) % NZ], recv.at[d], ss.at[d], rs.at[d], device(y, x, core, (z + d) % NZ)).start()
        recv[0] = send[z]

    def finish_along_z(send, recv, ss, rs, turned, slots):
        for d in FAR_FIRST:
            remote(send.at[0], recv.at[d], ss.at[d], rs.at[d], other_core).wait_recv()
        count = 4 * slots
        for half in range(2):
            blocks = swap_blocks([recv[half * 8 + a].astype(F32) for a in range(8)])
            for low in range(8):
                turned[half, low * count : low * count + count, :] = blocks[low]
        result = []
        for x_low in range(2):
            halves = []
            for half in range(2):
                starts = [part * slots + s for s in range(x_low, slots, 2) for part in range(4)]
                rows = [turned[half, pl.ds(start, 8, stride=count), :] for start in starts]
                halves.append(jnp.concatenate(rows, axis=0))
            result.append(jnp.concatenate(halves, axis=1).astype(BF16))
        return result

    def by_plane(side, first_slot, slots, rows, send):
        wait_along_x(side, first_slot, slots)
        for part in range(4):
            lanes = slice(part * 128, part * 128 + 128)
            block = x_recv[side, first_slot : first_slot + slots, :, lanes].astype(F32).reshape(slots * 16, 128)
            rows[part * slots * 16 : (part + 1) * slots * 16, :] = block
        for plane in range(NZ):
            send[plane] = rows[pl.ds(plane, 4 * slots, stride=16), :].astype(BF16)

    left_z = (left_send, left_recv, left_ss, left_rs)
    right_z = [(right_send.at[h], right_recv.at[h], right_ss.at[h], right_rs.at[h]) for h in range(2)]

    def send_left():
        by_plane(0, 0, 8, left_rows, left_send)
        start_along_z(*left_z)

    def send_right(h):
        by_plane(1, h * 4, 4, right_rows.at[h], right_send.at[h])
        start_along_z(*right_z[h])

    edges_of(1, w_b_gate, w_b_proj)
    pl.semaphore_wait(barrier, len(peers))
    for d in (4, 12):
        pl.semaphore_signal(ring_sem, inc=1, device_id=device(y, x, core, (z + d) % NZ), device_id_type=MESH)
    start_along_x(1)
    for load in loads[6:]:
        load.wait()
    edges_of(0, w_a_gate, w_a_proj)
    start_along_x(0)
    pl.semaphore_wait(ring_sem, 2)

    def after_both_cores(send, recv, ss, rs):
        d = FAR_FIRST[-1]
        remote(send.at[0], recv.at[d], ss.at[d], rs.at[d], other_core).wait_send()
        pl.semaphore_signal(core_sem, inc=1, device_id=other_core, device_id_type=MESH)
        pl.semaphore_wait(core_sem, 1)

    send_right(0)
    send_right(1)
    after_both_cores(*right_z[1])
    send_left()
    gate[...] = jax.nn.sigmoid(jnp.dot(normed[...], w_gate[...], preferred_element_type=F32))

    def right_of(of_y, h):
        return right_all.at[of_y % 2, h, :, pl.ds(pl.multiple_of((of_y // 2) * 64, 64), 64), :]

    def y_copy(h, d, of_y):
        return remote(right_of(y, h), right_of(of_y, h), y_ss.at[h, d], y_rs.at[h, d], device((y + d) % NY, x, core, z))

    def send_along_y(h):
        for x_low, rows in enumerate(finish_along_z(*right_z[h], right_turned.at[h], 4)):
            right_all[y % 2, h, x_low, pl.ds(pl.multiple_of((y // 2) * 64, 64), 64), :] = rows
        for d in ALONG_Y:
            y_copy(h, d, y).start()

    def back_z_copy(to_z):
        return remote(
            back_z_send.at[to_z], back_z_recv.at[z], back_z_ss.at[to_z], back_z_rs.at[z], device(y, x, core, to_z)
        )

    def contract(odd, h):
        for of_y in (odd, odd + 2):
            d = (y + NY - of_y) % NY

            @pl.when(d != 0)
            def _():
                y_copy(h, d, of_y).wait_recv()

        product[odd * 2 + h] = lax.dot_general(
            left[0], right_all[odd, h, 0], NT, preferred_element_type=F32
        ) + lax.dot_general(left[1], right_all[odd, h, 1], NT, preferred_element_type=F32)
        blocks = swap_blocks([product[odd * 2 + h, pl.ds(low, 16, stride=8), :] for low in range(8)])
        for low in range(8):
            back_z_send[odd * 8 + h * 4 + low % 4, low // 4] = blocks[low].astype(BF16)
        for to_z in range(odd * 8 + h * 4, odd * 8 + h * 4 + 4):

            @pl.when(z != to_z)
            def _():
                back_z_copy(to_z).start()

    send_along_y(0)
    send_along_y(1)
    for x_low, rows in enumerate(finish_along_z(*left_z, left_turned, 8)):
        left[x_low] = rows
    contract(0, 0)
    contract(0, 1)
    contract(1, 0)
    contract(1, 1)
    back_z_recv[z] = back_z_send[z]
    for d in FAR_FIRST:
        from_z = (z + NZ - d) % NZ
        remote(
            back_z_send.at[0], back_z_recv.at[from_z], back_z_ss.at[from_z], back_z_rs.at[from_z], other_core
        ).wait_recv()

    back_rows[...] = back_z_recv[...].astype(F32).reshape(512, 128)
    for to_core in range(2):
        for to_x in range(NX):
            start = (to_x % 2) * 16 + (to_x // 2) * 8 + to_core * 4
            rows = [back_rows[pl.ds(start + part, 16, stride=32), :] for part in range(4)]
            back_x_send[slot_of(to_x, to_core)] = jnp.concatenate(rows, axis=0).astype(BF16)
    back_x = [
        remote(back_x_send.at[slot_at(dx, dc)], back_x_recv.at[slot], back_x_ss.at[n], back_x_rs.at[n], x_peers[n])
        for n, (dx, dc) in enumerate(X_AND_CORE)
    ]
    for copy in back_x:
        copy.start()
    back_x_recv[slot] = back_x_send[slot]
    for n, (dx, dc) in enumerate(X_AND_CORE):
        arrived = back_x_recv.at[slot_at(-dx, dc)]
        remote(back_x_send.at[0], arrived, back_x_ss.at[n], back_x_rs.at[n], x_peers[n]).wait_recv()

    gain_col = jnp.broadcast_to(out_gain[...], (8, 128)).T[:, :1]
    bias_col = jnp.broadcast_to(out_bias[...], (8, 128)).T[:, :1]
    for part in range(4):
        contracted = back_x_recv[:, part * 16 : part * 16 + 16, :].astype(F32).reshape(128, 128)
        centred = contracted - jnp.mean(contracted, axis=0, keepdims=True)
        variance = jnp.mean(centred * centred, axis=0, keepdims=True)
        normed_out = (centred * lax.rsqrt(variance + 1e-05) * gain_col + bias_col).T.astype(BF16)
        result = gate[part * 128 : part * 128 + 128, :] * jnp.dot(normed_out, w_out[...], preferred_element_type=F32)
        out_ref[part * 8 : part * 8 + 8] = result.astype(BF16).reshape(8, 16, 128)

    for copy in back_x:
        copy.wait_send()
    for side in range(2):
        for n in range(len(X_AND_CORE)):
            remote(
                x_send.at[side, 0], x_recv.at[side, 0], x_ss.at[side, n], x_rs.at[side, n], other_core
            ).wait_send()
    def wait_sent(send, recv, ss, rs, distances):
        for d in distances:
            remote(send.at[0], recv.at[d], ss.at[d], rs.at[d], other_core).wait_send()

    wait_sent(*left_z, FAR_FIRST)
    wait_sent(*right_z[0], FAR_FIRST)
    wait_sent(*right_z[1], FAR_FIRST[:-1])
    for h in range(2):
        for d in ALONG_Y:
            y_copy(h, d, y).wait_send()
    for d in FAR_FIRST:
        back_z_copy((z + d) % NZ).wait_send()


def per_device(
    pair, pair_mask, norm_gain, norm_bias, w_a_gate, w_a_proj, w_b_gate, w_b_proj, w_gate, out_gain, out_bias, w_out
):
    args = (
        pair, pair_mask.T, norm_gain.reshape(1, 128), norm_bias.reshape(1, 128), w_a_gate, w_a_proj, w_b_gate, w_b_proj,
        w_gate, out_gain.reshape(1, 128), out_bias.reshape(1, 128), w_out,
    )
    dma = pltpu.SemaphoreType.DMA
    return pl.pallas_call(
        kernel,
        out_shape=pltpu.VMEM(pair.shape, BF16),
        in_specs=[pl.BlockSpec(memory_space=pl.ANY)] * len(args),
        out_specs=pl.BlockSpec(memory_space=pltpu.VMEM),
        scratch_shapes=[pltpu.VMEM(a.shape, a.dtype) for a in args]
        + [
            pltpu.VMEM((512, 128), BF16),
            pltpu.VMEM((512, 128), F32),
            pltpu.VMEM((2, 8, 16, 512), BF16),
            pltpu.VMEM((2, 8, 16, 512), BF16),
            pltpu.VMEM((512, 128), F32),
            pltpu.VMEM((2, 256, 128), F32),
            pltpu.VMEM((16, 32, 128), BF16),
            pltpu.VMEM((16, 32, 128), BF16),
            pltpu.VMEM((2, 16, 16, 128), BF16),
            pltpu.VMEM((2, 16, 16, 128), BF16),
            pltpu.VMEM((2, 256, 128), F32),
            pltpu.VMEM((2, 2, 128, 128), F32),
            pltpu.VMEM((2, 128, 256), BF16),
            pltpu.VMEM((2, 2, 2, 128, 256), BF16),
            pltpu.VMEM((4, 128, 128), F32),
            pltpu.VMEM((16, 2, 16, 128), BF16),
            pltpu.VMEM((16, 2, 16, 128), BF16),
            pltpu.VMEM((512, 128), F32),
            pltpu.VMEM((8, 64, 128), BF16),
            pltpu.VMEM((8, 64, 128), BF16),
            dma((12,)), dma((2, 7)), dma((2, 7)), dma((16,)), dma((16,)), dma((2, 16)), dma((2, 16)), dma((2, 4)),
            dma((2, 4)), dma((16,)), dma((16,)), dma((7,)), dma((7,)), pltpu.SemaphoreType.REGULAR, pltpu.SemaphoreType.REGULAR,
        ],
        compiler_params=pltpu.CompilerParams(collective_id=0, has_side_effects=True, vmem_limit_bytes=32 << 20),
        name="triangle",
    )(*[pltpu.with_memory_space_constraint(a, pltpu.HBM) for a in args])


def solution(mesh):
    return jax.shard_map(
        per_device,
        mesh=mesh,
        in_specs=(P("row", "col", None), P("row", "col")) + (P(),) * 10,
        out_specs=P("row", "col", None),
        check_vma=False,
    )
```

```python
import jax
import jax.numpy as jnp
from jax import lax
from jax.experimental import pallas as pl
from jax.experimental.pallas import tpu as pltpu
from jax.sharding import PartitionSpec as P

MESH = pl.DeviceIdType.MESH
F32, BF16 = jnp.float32, jnp.bfloat16
NZ, NX, NY = 16, 4, 4
FAR_FIRST = (8, 7, 9, 6, 10, 5, 11, 4, 12, 3, 13, 2, 14, 1, 15)
NEAR = (4, 12, 3, 13, 2, 14, 1, 15)
STEP = 14
ALONG_Y = (2, 1, 3)
X_AND_CORE = tuple((dx, dc) for dx in (2, 1, 3, 0) for dc in (1, 0) if dx or dc)
NT = (((1,), (1,)), ((), ()))
TN = (((0,), (0,)), ((), ()))


def swap_blocks(arrays):
    arrays = list(arrays)
    lane = lax.broadcasted_iota(jnp.int32, arrays[0].shape, 1)
    for bit in range(3):
        step = 1 << bit
        upper = ((lane // 16) // step) % 2 == 1
        for a in range(8):
            if not a & step:
                low, high = arrays[a], arrays[a | step]
                arrays[a] = jnp.where(upper, pltpu.roll(high, 16 * step, 1), low)
                arrays[a | step] = jnp.where(upper, high, pltpu.roll(low, 128 - 16 * step, 1))
    return arrays


def kernel(
    pair_hbm, mask_hbm, norm_gain_hbm, norm_bias_hbm, w_a_gate_hbm, w_a_proj_hbm, w_b_gate_hbm, w_b_proj_hbm,
    w_gate_hbm, out_gain_hbm, out_bias_hbm, w_out_hbm,
    out_ref,
    pair, mask, norm_gain, norm_bias, w_a_gate, w_a_proj, w_b_gate, w_b_proj, w_gate, out_gain, out_bias, w_out,
    normed, gate, x_send, x_recv, left_rows, right_rows, left_send, left_recv, right_send, right_recv, left_turned,
    right_turned, left, right_all, product, back_z_send, back_z_recv, back_rows, back_x_send, back_x_recv,
    in_sem, x_ss, x_rs, left_ss, left_rs, right_ss, right_rs, y_ss, y_rs, back_z_ss, back_z_rs, back_x_ss, back_x_rs,
    ring_sem, core_sem, wave_sem,
):
    row, col = lax.axis_index("row"), lax.axis_index("col")
    y, core = row // 4, row % 2
    x = ((row // 2) % 2) * 2 + col // 16
    z = col % 16

    def device(y, x, core, z):
        return {"row": y * 4 + (x // 2) * 2 + core, "col": (x % 2) * 16 + z}

    def slot_of(x, core):
        return (x // 2) * 4 + core * 2 + x % 2

    def slot_at(dx, dc):
        return slot_of((x + dx + NX) % NX, (core + dc) % 2)

    def remote(src, dst, ss, rs, to):
        return pltpu.make_async_remote_copy(
            src_ref=src, dst_ref=dst, send_sem=ss, recv_sem=rs, device_id=to, device_id_type=MESH
        )

    slot = slot_of(x, core)
    other_core = device(y, x, 1 - core, z)
    x_peers = [device(y, (x + dx) % NX, (core + dc) % 2, z) for dx, dc in X_AND_CORE]
    y_peers = [device((y + d) % NY, x, core, z) for d in ALONG_Y]
    barrier = pltpu.get_barrier_semaphore()
    peers = [device(y, x, core, (z + d) % NZ) for d in NEAR] + x_peers + y_peers
    for peer in peers:
        pl.semaphore_signal(barrier, inc=1, device_id=peer, device_id_type=MESH)

    loads = [
        pltpu.make_async_copy(src, dst, in_sem.at[n])
        for n, (src, dst) in enumerate(
            (
                (pair_hbm, pair), (norm_gain_hbm, norm_gain), (norm_bias_hbm, norm_bias), (w_b_gate_hbm, w_b_gate),
                (w_b_proj_hbm, w_b_proj), (mask_hbm, mask), (w_a_gate_hbm, w_a_gate), (w_a_proj_hbm, w_a_proj),
                (w_gate_hbm, w_gate), (out_gain_hbm, out_gain), (out_bias_hbm, out_bias), (w_out_hbm, w_out),
            )
        )
    ]
    for load in loads:
        load.start()
    for load in loads[:6]:
        load.wait()

    values = pair[...].astype(F32).reshape(512, 128)
    centred = values - jnp.mean(values, axis=1, keepdims=True)
    variance = jnp.mean(centred * centred, axis=1, keepdims=True)
    normed[...] = (centred * lax.rsqrt(variance + 1e-05) * norm_gain[...] + norm_bias[...]).astype(BF16)

    at_col = lax.broadcasted_iota(jnp.int32, (16, 512), 1) % 16 == lax.broadcasted_iota(jnp.int32, (16, 512), 0)
    at_row = lax.broadcasted_iota(jnp.int32, (32, 512), 1) // 16 == lax.broadcasted_iota(jnp.int32, (32, 512), 0)
    spread = lax.dot_general(
        mask[...].astype(F32).astype(BF16), at_col.astype(F32).astype(BF16), TN, preferred_element_type=F32
    )
    mask_row = jnp.sum(jnp.where(at_row, spread, 0.0), axis=0, keepdims=True)

    def project(weight):
        turned_weight = weight[...].astype(F32).T.astype(BF16)
        return lax.dot_general(turned_weight, normed[...], NT, preferred_element_type=F32)

    def edges_of(side, w_gate, w_proj):
        edges = mask_row * jax.nn.sigmoid(project(w_gate)) * project(w_proj)
        x_send[side] = edges.reshape(8, 16, 512).astype(BF16)

    def start_along_x(side):
        for n, (dx, dc) in enumerate(X_AND_CORE):
            remote(
                x_send.at[side, slot_at(dx, dc)], x_recv.at[side, slot], x_ss.at[side, n], x_rs.at[side, n], x_peers[n]
            ).start()
        x_recv[side, slot] = x_send[side, slot]

    def wait_along_x(side, first_slot, slots):
        for n, (dx, dc) in enumerate(X_AND_CORE):
            source = slot_at(-dx, dc)

            def wait():
                remote(
                    x_send.at[side, 0], x_recv.at[side, source], x_ss.at[side, n], x_rs.at[side, n], other_core
                ).wait_recv()

            if slots == 8:
                wait()
            else:
                pl.when(source // 4 == first_slot // 4)(wait)

    def start_along_z(send, recv, ss, rs):
        for d in FAR_FIRST:
            remote(send.at[(z + d) % NZ], recv.at[d], ss.at[d], rs.at[d], device(y, x, core, (z + d) % NZ)).start()
        recv[0] = send[z]

    def finish_along_z(send, recv, ss, rs, turned, slots):
        for d in FAR_FIRST:
            remote(send.at[0], recv.at[d], ss.at[d], rs.at[d], other_core).wait_recv()
        count = 4 * slots
        for half in range(2):
            blocks = swap_blocks([recv[half * 8 + a].astype(F32) for a in range(8)])
            for low in range(8):
                turned[half, low * count : low * count + count, :] = blocks[low]
        result = []
        for x_low in range(2):
            halves = []
            for half in range(2):
                starts = [part * slots + s for s in range(x_low, slots, 2) for part in range(4)]
                rows = [turned[half, pl.ds(start, 8, stride=count), :] for start in starts]
                halves.append(jnp.concatenate(rows, axis=0))
            result.append(jnp.concatenate(halves, axis=1).astype(BF16))
        return result

    def by_plane(side, first_slot, slots, rows, send):
        wait_along_x(side, first_slot, slots)
        for part in range(4):
            lanes = slice(part * 128, part * 128 + 128)
            block = x_recv[side, first_slot : first_slot + slots, :, lanes].astype(F32).reshape(slots * 16, 128)
            rows[part * slots * 16 : (part + 1) * slots * 16, :] = block
        for plane in range(NZ):
            send[plane] = rows[pl.ds(plane, 4 * slots, stride=16), :].astype(BF16)

    left_z = (left_send, left_recv, left_ss, left_rs)
    right_z = [(right_send.at[h], right_recv.at[h], right_ss.at[h], right_rs.at[h]) for h in range(2)]

    def send_left():
        by_plane(0, 0, 8, left_rows, left_send)
        start_along_z(*left_z)

    def send_right(h):
        by_plane(1, h * 4, 4, right_rows.at[h], right_send.at[h])
        start_along_z(*right_z[h])

    edges_of(1, w_b_gate, w_b_proj)
    pl.semaphore_wait(barrier, len(peers))
    for d in (4, 12):
        pl.semaphore_signal(ring_sem, inc=1, device_id=device(y, x, core, (z + d) % NZ), device_id_type=MESH)
    start_along_x(1)
    for load in loads[6:]:
        load.wait()
    edges_of(0, w_a_gate, w_a_proj)
    start_along_x(0)
    pl.semaphore_wait(ring_sem, 2)

    def wait_sent(send, recv, ss, rs, distances):
        for d in distances:
            remote(send.at[0], recv.at[d], ss.at[d], rs.at[d], other_core).wait_send()

    def after_both_cores(send, recv, ss, rs):
        d = FAR_FIRST[STEP]
        remote(send.at[0], recv.at[d], ss.at[d], rs.at[d], other_core).wait_send()
        pl.semaphore_signal(core_sem, inc=1, device_id=other_core, device_id_type=MESH)
        pl.semaphore_wait(core_sem, 1)

    send_right(0)
    send_right(1)
    after_both_cores(*right_z[0])
    send_left()
    gate[...] = jax.nn.sigmoid(jnp.dot(normed[...], w_gate[...], preferred_element_type=F32))

    def right_of(of_y, h):
        return right_all.at[of_y % 2, h, :, pl.ds(pl.multiple_of((of_y // 2) * 64, 64), 64), :]

    def y_copy(h, d, of_y):
        return remote(right_of(y, h), right_of(of_y, h), y_ss.at[h, d], y_rs.at[h, d], device((y + d) % NY, x, core, z))

    def send_along_y(h):
        for x_low, rows in enumerate(finish_along_z(*right_z[h], right_turned.at[h], 4)):
            right_all[y % 2, h, x_low, pl.ds(pl.multiple_of((y // 2) * 64, 64), 64), :] = rows
        for d in ALONG_Y:
            y_copy(h, d, y).start()

    def back_z_copy(to_z):
        return remote(
            back_z_send.at[to_z], back_z_recv.at[z], back_z_ss.at[to_z], back_z_rs.at[z], device(y, x, core, to_z)
        )

    def wait_along_y(odd, h):
        for of_y in (odd, odd + 2):
            d = (y + NY - of_y) % NY

            @pl.when(d != 0)
            def _():
                y_copy(h, d, of_y).wait_recv()

    def contract(odd, h):
        if odd or h:
            wait_along_y(odd, h)
        product[odd * 2 + h] = lax.dot_general(
            left[0], right_all[odd, h, 0], NT, preferred_element_type=F32
        ) + lax.dot_general(left[1], right_all[odd, h, 1], NT, preferred_element_type=F32)
        blocks = swap_blocks([product[odd * 2 + h, pl.ds(low, 16, stride=8), :] for low in range(8)])
        for low in range(8):
            back_z_send[odd * 8 + h * 4 + low % 4, low // 4] = blocks[low].astype(BF16)
        for to_z in range(odd * 8 + h * 4, odd * 8 + h * 4 + 4):

            @pl.when(z != to_z)
            def _():
                back_z_copy(to_z).start()

    @pl.when(y % 2 == 0)
    def _():
        send_along_y(0)
        send_along_y(1)

    wait_along_y(0, 0)

    @pl.when(y % 2 == 1)
    def _():
        send_along_y(0)
        send_along_y(1)

    for x_low, rows in enumerate(finish_along_z(*left_z, left_turned, 8)):
        left[x_low] = rows
    contract(0, 0)

    first = jnp.where(z == 0, 1, 0)
    back_z_copy(first).wait_send()
    pl.semaphore_signal(wave_sem, inc=1, device_id=other_core, device_id_type=MESH)
    pl.semaphore_wait(wave_sem, 1)
    contract(0, 1)
    contract(1, 0)
    contract(1, 1)
    for side in range(2):
        for n in range(len(X_AND_CORE)):
            remote(
                x_send.at[side, 0], x_recv.at[side, 0], x_ss.at[side, n], x_rs.at[side, n], other_core
            ).wait_send()
    wait_sent(*left_z, FAR_FIRST)
    wait_sent(*right_z[1], FAR_FIRST)
    wait_sent(*right_z[0], FAR_FIRST[:STEP] + FAR_FIRST[STEP + 1 :])
    for h in range(2):
        for d in ALONG_Y:
            y_copy(h, d, y).wait_send()

    back_z_recv[z] = back_z_send[z]
    for d in FAR_FIRST:
        from_z = (z + NZ - d) % NZ
        remote(
            back_z_send.at[0], back_z_recv.at[from_z], back_z_ss.at[from_z], back_z_rs.at[from_z], other_core
        ).wait_recv()

    back_rows[...] = back_z_recv[...].astype(F32).reshape(512, 128)
    for to_core in range(2):
        for to_x in range(NX):
            start = (to_x % 2) * 16 + (to_x // 2) * 8 + to_core * 4
            rows = [back_rows[pl.ds(start + part, 16, stride=32), :] for part in range(4)]
            back_x_send[slot_of(to_x, to_core)] = jnp.concatenate(rows, axis=0).astype(BF16)
    back_x = [
        remote(back_x_send.at[slot_at(dx, dc)], back_x_recv.at[slot], back_x_ss.at[n], back_x_rs.at[n], x_peers[n])
        for n, (dx, dc) in enumerate(X_AND_CORE)
    ]
    for copy in back_x:
        copy.start()
    gain_col = jnp.broadcast_to(out_gain[...], (8, 128)).T[:, :1]
    bias_col = jnp.broadcast_to(out_bias[...], (8, 128)).T[:, :1]
    back_x_recv[slot] = back_x_send[slot]
    for d in FAR_FIRST:
        to_z = (z + d) % NZ
        pl.when(to_z != first)(lambda: back_z_copy(to_z).wait_send())
    for n, (dx, dc) in enumerate(X_AND_CORE):
        arrived = back_x_recv.at[slot_at(-dx, dc)]
        remote(back_x_send.at[0], arrived, back_x_ss.at[n], back_x_rs.at[n], x_peers[n]).wait_recv()

    for part in range(4):
        contracted = back_x_recv[:, part * 16 : part * 16 + 16, :].astype(F32).reshape(128, 128)
        centred = contracted - jnp.mean(contracted, axis=0, keepdims=True)
        variance = jnp.mean(centred * centred, axis=0, keepdims=True)
        normed_out = (centred * lax.rsqrt(variance + 1e-05) * gain_col + bias_col).T.astype(BF16)
        result = gate[part * 128 : part * 128 + 128, :] * jnp.dot(normed_out, w_out[...], preferred_element_type=F32)
        out_ref[part * 8 : part * 8 + 8] = result.astype(BF16).reshape(8, 16, 128)

    for copy in back_x:
        copy.wait_send()


def per_device(
    pair, pair_mask, norm_gain, norm_bias, w_a_gate, w_a_proj, w_b_gate, w_b_proj, w_gate, out_gain, out_bias, w_out
):
    args = (
        pair, pair_mask.T, norm_gain.reshape(1, 128), norm_bias.reshape(1, 128), w_a_gate, w_a_proj, w_b_gate, w_b_proj,
        w_gate, out_gain.reshape(1, 128), out_bias.reshape(1, 128), w_out,
    )
    dma = pltpu.SemaphoreType.DMA
    return pl.pallas_call(
        kernel,
        out_shape=pltpu.VMEM(pair.shape, BF16),
        in_specs=[pl.BlockSpec(memory_space=pl.ANY)] * len(args),
        out_specs=pl.BlockSpec(memory_space=pltpu.VMEM),
        scratch_shapes=[pltpu.VMEM(a.shape, a.dtype) for a in args]
        + [
            pltpu.VMEM((512, 128), BF16),
            pltpu.VMEM((512, 128), F32),
            pltpu.VMEM((2, 8, 16, 512), BF16),
            pltpu.VMEM((2, 8, 16, 512), BF16),
            pltpu.VMEM((512, 128), F32),
            pltpu.VMEM((2, 256, 128), F32),
            pltpu.VMEM((16, 32, 128), BF16),
            pltpu.VMEM((16, 32, 128), BF16),
            pltpu.VMEM((2, 16, 16, 128), BF16),
            pltpu.VMEM((2, 16, 16, 128), BF16),
            pltpu.VMEM((2, 256, 128), F32),
            pltpu.VMEM((2, 2, 128, 128), F32),
            pltpu.VMEM((2, 128, 256), BF16),
            pltpu.VMEM((2, 2, 2, 128, 256), BF16),
            pltpu.VMEM((4, 128, 128), F32),
            pltpu.VMEM((16, 2, 16, 128), BF16),
            pltpu.VMEM((16, 2, 16, 128), BF16),
            pltpu.VMEM((512, 128), F32),
            pltpu.VMEM((8, 64, 128), BF16),
            pltpu.VMEM((8, 64, 128), BF16),
            dma((12,)), dma((2, 7)), dma((2, 7)), dma((16,)), dma((16,)), dma((2, 16)), dma((2, 16)), dma((2, 4)),
            dma((2, 4)), dma((16,)), dma((16,)), dma((7,)), dma((7,)), pltpu.SemaphoreType.REGULAR, pltpu.SemaphoreType.REGULAR,
            pltpu.SemaphoreType.REGULAR,
        ],
        compiler_params=pltpu.CompilerParams(collective_id=0, has_side_effects=True, vmem_limit_bytes=32 << 20),
        name="triangle",
    )(*[pltpu.with_memory_space_constraint(a, pltpu.HBM) for a in args])


def solution(mesh):
    return jax.shard_map(
        per_device,
        mesh=mesh,
        in_specs=(P("row", "col", None), P("row", "col")) + (P(),) * 10,
        out_specs=P("row", "col", None),
        check_vma=False,
    )
```

```python
import jax
import jax.numpy as jnp
from jax import lax
from jax.experimental import pallas as pl
from jax.experimental.pallas import tpu as pltpu
from jax.sharding import PartitionSpec as P

MESH = pl.DeviceIdType.MESH
F32, BF16 = jnp.float32, jnp.bfloat16
NZ, NX, NY = 16, 4, 4
FAR_FIRST = (8, 7, 9, 6, 10, 5, 11, 4, 12, 3, 13, 2, 14, 1, 15)
NEAR = (4, 12, 3, 13, 2, 14, 1, 15)
STEP = 14
ALONG_Y = (2, 1, 3)
X_AND_CORE = tuple((dx, dc) for dx in (2, 1, 3, 0) for dc in (1, 0) if dx or dc)
NT = (((1,), (1,)), ((), ()))
TN = (((0,), (0,)), ((), ()))


def swap_blocks(arrays):
    arrays = list(arrays)
    lane = lax.broadcasted_iota(jnp.int32, arrays[0].shape, 1)
    for bit in range(3):
        step = 1 << bit
        upper = ((lane // 16) // step) % 2 == 1
        for a in range(8):
            if not a & step:
                low, high = arrays[a], arrays[a | step]
                arrays[a] = jnp.where(upper, pltpu.roll(high, 16 * step, 1), low)
                arrays[a | step] = jnp.where(upper, high, pltpu.roll(low, 128 - 16 * step, 1))
    return arrays


def kernel(
    pair_hbm, mask_hbm, norm_gain_hbm, norm_bias_hbm, w_a_gate_hbm, w_a_proj_hbm, w_b_gate_hbm, w_b_proj_hbm,
    w_gate_hbm, out_gain_hbm, out_bias_hbm, w_out_hbm,
    out_ref,
    pair, mask, norm_gain, norm_bias, w_a_gate, w_a_proj, w_b_gate, w_b_proj, w_gate, out_gain, out_bias, w_out,
    normed, gate, x_send, x_recv, left_rows, right_rows, left_send, left_recv, right_send, right_recv, left_turned,
    right_turned, left, right_all, product, back_z_send, back_z_recv, back_rows, back_x_send, back_x_recv,
    in_sem, x_ss, x_rs, left_ss, left_rs, right_ss, right_rs, y_ss, y_rs, back_z_ss, back_z_rs, back_x_ss, back_x_rs,
    ring_sem, core_sem, wave_sem,
):
    row, col = lax.axis_index("row"), lax.axis_index("col")
    y, core = row // 4, row % 2
    x = ((row // 2) % 2) * 2 + col // 16
    z = col % 16

    def device(y, x, core, z):
        return {"row": y * 4 + (x // 2) * 2 + core, "col": (x % 2) * 16 + z}

    def slot_of(x, core):
        return (x // 2) * 4 + core * 2 + x % 2

    def slot_at(dx, dc):
        return slot_of((x + dx + NX) % NX, (core + dc) % 2)

    def remote(src, dst, ss, rs, to):
        return pltpu.make_async_remote_copy(
            src_ref=src, dst_ref=dst, send_sem=ss, recv_sem=rs, device_id=to, device_id_type=MESH
        )

    slot = slot_of(x, core)
    other_core = device(y, x, 1 - core, z)
    x_peers = [device(y, (x + dx) % NX, (core + dc) % 2, z) for dx, dc in X_AND_CORE]
    y_peers = [device((y + d) % NY, x, core, z) for d in ALONG_Y]
    barrier = pltpu.get_barrier_semaphore()
    peers = [device(y, x, core, (z + d) % NZ) for d in NEAR] + x_peers + y_peers
    for peer in peers:
        pl.semaphore_signal(barrier, inc=1, device_id=peer, device_id_type=MESH)

    loads = [
        pltpu.make_async_copy(src, dst, in_sem.at[n])
        for n, (src, dst) in enumerate(
            (
                (pair_hbm, pair), (norm_gain_hbm, norm_gain), (norm_bias_hbm, norm_bias), (w_b_gate_hbm, w_b_gate),
                (w_b_proj_hbm, w_b_proj), (mask_hbm, mask), (w_a_gate_hbm, w_a_gate), (w_a_proj_hbm, w_a_proj),
                (w_gate_hbm, w_gate), (out_gain_hbm, out_gain), (out_bias_hbm, out_bias), (w_out_hbm, w_out),
            )
        )
    ]
    for load in loads:
        load.start()
    for load in loads[:3]:
        load.wait()

    values = pair[...].astype(F32).reshape(512, 128)
    centred = values - jnp.mean(values, axis=1, keepdims=True)
    variance = jnp.mean(centred * centred, axis=1, keepdims=True)
    normed[...] = (centred * lax.rsqrt(variance + 1e-05) * norm_gain[...] + norm_bias[...]).astype(BF16)

    for load in loads[3:6]:
        load.wait()

    at_col = lax.broadcasted_iota(jnp.int32, (16, 512), 1) % 16 == lax.broadcasted_iota(jnp.int32, (16, 512), 0)
    at_row = lax.broadcasted_iota(jnp.int32, (32, 512), 1) // 16 == lax.broadcasted_iota(jnp.int32, (32, 512), 0)
    spread = lax.dot_general(
        mask[...].astype(F32).astype(BF16), at_col.astype(F32).astype(BF16), TN, preferred_element_type=F32
    )
    mask_row = jnp.sum(jnp.where(at_row, spread, 0.0), axis=0, keepdims=True)

    def project(weight):
        turned_weight = weight[...].astype(F32).T.astype(BF16)
        return lax.dot_general(turned_weight, normed[...], NT, preferred_element_type=F32)

    def edges_of(side, w_gate, w_proj):
        edges = mask_row * jax.nn.sigmoid(project(w_gate)) * project(w_proj)
        x_send[side] = edges.reshape(8, 16, 512).astype(BF16)

    def start_along_x(side):
        for n, (dx, dc) in enumerate(X_AND_CORE):
            remote(
                x_send.at[side, slot_at(dx, dc)], x_recv.at[side, slot], x_ss.at[side, n], x_rs.at[side, n], x_peers[n]
            ).start()
        x_recv[side, slot] = x_send[side, slot]

    def wait_along_x(side, first_slot, slots):
        for n, (dx, dc) in enumerate(X_AND_CORE):
            source = slot_at(-dx, dc)

            def wait():
                remote(
                    x_send.at[side, 0], x_recv.at[side, source], x_ss.at[side, n], x_rs.at[side, n], other_core
                ).wait_recv()

            if slots == 8:
                wait()
            else:
                pl.when(source // 4 == first_slot // 4)(wait)

    def start_along_z(send, recv, ss, rs):
        for d in FAR_FIRST:
            remote(send.at[(z + d) % NZ], recv.at[d], ss.at[d], rs.at[d], device(y, x, core, (z + d) % NZ)).start()
        recv[0] = send[z]

    def finish_along_z(send, recv, ss, rs, turned, slots):
        for d in FAR_FIRST:
            remote(send.at[0], recv.at[d], ss.at[d], rs.at[d], other_core).wait_recv()
        count = 4 * slots
        for half in range(2):
            blocks = swap_blocks([recv[half * 8 + a].astype(F32) for a in range(8)])
            for low in range(8):
                turned[half, low * count : low * count + count, :] = blocks[low]
        result = []
        for x_low in range(2):
            halves = []
            for half in range(2):
                starts = [part * slots + s for s in range(x_low, slots, 2) for part in range(4)]
                rows = [turned[half, pl.ds(start, 8, stride=count), :] for start in starts]
                halves.append(jnp.concatenate(rows, axis=0))
            result.append(jnp.concatenate(halves, axis=1).astype(BF16))
        return result

    def by_plane(side, first_slot, slots, rows, send):
        wait_along_x(side, first_slot, slots)
        for part in range(4):
            lanes = slice(part * 128, part * 128 + 128)
            block = x_recv[side, first_slot : first_slot + slots, :, lanes].astype(F32).reshape(slots * 16, 128)
            rows[part * slots * 16 : (part + 1) * slots * 16, :] = block
        for plane in range(NZ):
            send[plane] = rows[pl.ds(plane, 4 * slots, stride=16), :].astype(BF16)

    left_z = (left_send, left_recv, left_ss, left_rs)
    right_z = [(right_send.at[h], right_recv.at[h], right_ss.at[h], right_rs.at[h]) for h in range(2)]

    def send_left():
        by_plane(0, 0, 8, left_rows, left_send)
        start_along_z(*left_z)

    def send_right(h):
        by_plane(1, h * 4, 4, right_rows.at[h], right_send.at[h])
        start_along_z(*right_z[h])

    edges_of(1, w_b_gate, w_b_proj)
    pl.semaphore_wait(barrier, len(peers))
    for d in (4, 12):
        pl.semaphore_signal(ring_sem, inc=1, device_id=device(y, x, core, (z + d) % NZ), device_id_type=MESH)
    start_along_x(1)
    for load in loads[6:]:
        load.wait()
    edges_of(0, w_a_gate, w_a_proj)
    pl.semaphore_wait(ring_sem, 2)

    def wait_sent(send, recv, ss, rs, distances):
        for d in distances:
            remote(send.at[0], recv.at[d], ss.at[d], rs.at[d], other_core).wait_send()

    def after_both_cores(send, recv, ss, rs):
        d = FAR_FIRST[STEP]
        remote(send.at[0], recv.at[d], ss.at[d], rs.at[d], other_core).wait_send()
        pl.semaphore_signal(core_sem, inc=1, device_id=other_core, device_id_type=MESH)
        pl.semaphore_wait(core_sem, 1)

    send_right(0)
    start_along_x(0)
    send_right(1)
    after_both_cores(*right_z[0])
    send_left()
    gate[...] = jax.nn.sigmoid(jnp.dot(normed[...], w_gate[...], preferred_element_type=F32))

    def right_of(of_y, h):
        return right_all.at[of_y % 2, h, :, pl.ds(pl.multiple_of((of_y // 2) * 64, 64), 64), :]

    def y_copy(h, d, of_y):
        return remote(right_of(y, h), right_of(of_y, h), y_ss.at[h, d], y_rs.at[h, d], device((y + d) % NY, x, core, z))

    def send_along_y(h):
        for x_low, rows in enumerate(finish_along_z(*right_z[h], right_turned.at[h], 4)):
            right_all[y % 2, h, x_low, pl.ds(pl.multiple_of((y // 2) * 64, 64), 64), :] = rows
        for d in ALONG_Y:
            y_copy(h, d, y).start()

    def back_z_copy(to_z):
        return remote(
            back_z_send.at[to_z], back_z_recv.at[z], back_z_ss.at[to_z], back_z_rs.at[z], device(y, x, core, to_z)
        )

    def wait_along_y(odd, h):
        for of_y in (odd, odd + 2):
            d = (y + NY - of_y) % NY

            @pl.when(d != 0)
            def _():
                y_copy(h, d, of_y).wait_recv()

    def contract(odd, h):
        if odd or h:
            wait_along_y(odd, h)
        product[odd * 2 + h] = lax.dot_general(
            left[0], right_all[odd, h, 0], NT, preferred_element_type=F32
        ) + lax.dot_general(left[1], right_all[odd, h, 1], NT, preferred_element_type=F32)
        blocks = swap_blocks([product[odd * 2 + h, pl.ds(low, 16, stride=8), :] for low in range(8)])
        for low in range(8):
            back_z_send[odd * 8 + h * 4 + low % 4, low // 4] = blocks[low].astype(BF16)
        for to_z in range(odd * 8 + h * 4, odd * 8 + h * 4 + 4):

            @pl.when(z != to_z)
            def _():
                back_z_copy(to_z).start()

    @pl.when(y % 2 == 0)
    def _():
        send_along_y(0)
        send_along_y(1)

    wait_along_y(0, 0)

    @pl.when(y % 2 == 1)
    def _():
        send_along_y(0)
        send_along_y(1)

    for x_low, rows in enumerate(finish_along_z(*left_z, left_turned, 8)):
        left[x_low] = rows
    contract(0, 0)

    first = jnp.where(z == 0, 1, 0)
    back_z_copy(first).wait_send()
    pl.semaphore_signal(wave_sem, inc=1, device_id=other_core, device_id_type=MESH)
    pl.semaphore_wait(wave_sem, 1)
    contract(0, 1)
    contract(1, 0)
    contract(1, 1)
    for side in range(2):
        for n in range(len(X_AND_CORE)):
            remote(
                x_send.at[side, 0], x_recv.at[side, 0], x_ss.at[side, n], x_rs.at[side, n], other_core
            ).wait_send()
    wait_sent(*left_z, FAR_FIRST)
    wait_sent(*right_z[1], FAR_FIRST)
    wait_sent(*right_z[0], FAR_FIRST[:STEP] + FAR_FIRST[STEP + 1 :])
    for h in range(2):
        for d in ALONG_Y:
            y_copy(h, d, y).wait_send()

    back_z_recv[z] = back_z_send[z]
    for d in FAR_FIRST:
        from_z = (z + NZ - d) % NZ
        remote(
            back_z_send.at[0], back_z_recv.at[from_z], back_z_ss.at[from_z], back_z_rs.at[from_z], other_core
        ).wait_recv()

    back_rows[...] = back_z_recv[...].astype(F32).reshape(512, 128)
    for to_core in range(2):
        for to_x in range(NX):
            start = (to_x % 2) * 16 + (to_x // 2) * 8 + to_core * 4
            rows = [back_rows[pl.ds(start + part, 16, stride=32), :] for part in range(4)]
            back_x_send[slot_of(to_x, to_core)] = jnp.concatenate(rows, axis=0).astype(BF16)
    back_x = [
        remote(back_x_send.at[slot_at(dx, dc)], back_x_recv.at[slot], back_x_ss.at[n], back_x_rs.at[n], x_peers[n])
        for n, (dx, dc) in enumerate(X_AND_CORE)
    ]
    for copy in back_x:
        copy.start()
    gain_col = jnp.broadcast_to(out_gain[...], (8, 128)).T[:, :1]
    bias_col = jnp.broadcast_to(out_bias[...], (8, 128)).T[:, :1]
    back_x_recv[slot] = back_x_send[slot]
    for d in FAR_FIRST:
        to_z = (z + d) % NZ
        pl.when(to_z != first)(lambda: back_z_copy(to_z).wait_send())
    for n, (dx, dc) in enumerate(X_AND_CORE):
        arrived = back_x_recv.at[slot_at(-dx, dc)]
        remote(back_x_send.at[0], arrived, back_x_ss.at[n], back_x_rs.at[n], x_peers[n]).wait_recv()

    for part in range(4):
        contracted = back_x_recv[:, part * 16 : part * 16 + 16, :].astype(F32).reshape(128, 128)
        centred = contracted - jnp.mean(contracted, axis=0, keepdims=True)
        variance = jnp.mean(centred * centred, axis=0, keepdims=True)
        normed_out = (centred * lax.rsqrt(variance + 1e-05) * gain_col + bias_col).T.astype(BF16)
        result = gate[part * 128 : part * 128 + 128, :] * jnp.dot(normed_out, w_out[...], preferred_element_type=F32)
        out_ref[part * 8 : part * 8 + 8] = result.astype(BF16).reshape(8, 16, 128)

    for copy in back_x:
        copy.wait_send()


def per_device(
    pair, pair_mask, norm_gain, norm_bias, w_a_gate, w_a_proj, w_b_gate, w_b_proj, w_gate, out_gain, out_bias, w_out
):
    args = (
        pair, pair_mask.T, norm_gain.reshape(1, 128), norm_bias.reshape(1, 128), w_a_gate, w_a_proj, w_b_gate, w_b_proj,
        w_gate, out_gain.reshape(1, 128), out_bias.reshape(1, 128), w_out,
    )
    dma = pltpu.SemaphoreType.DMA
    return pl.pallas_call(
        kernel,
        out_shape=pltpu.VMEM(pair.shape, BF16),
        in_specs=[pl.BlockSpec(memory_space=pl.ANY)] * len(args),
        out_specs=pl.BlockSpec(memory_space=pltpu.VMEM),
        scratch_shapes=[pltpu.VMEM(a.shape, a.dtype) for a in args]
        + [
            pltpu.VMEM((512, 128), BF16),
            pltpu.VMEM((512, 128), F32),
            pltpu.VMEM((2, 8, 16, 512), BF16),
            pltpu.VMEM((2, 8, 16, 512), BF16),
            pltpu.VMEM((512, 128), F32),
            pltpu.VMEM((2, 256, 128), F32),
            pltpu.VMEM((16, 32, 128), BF16),
            pltpu.VMEM((16, 32, 128), BF16),
            pltpu.VMEM((2, 16, 16, 128), BF16),
            pltpu.VMEM((2, 16, 16, 128), BF16),
            pltpu.VMEM((2, 256, 128), F32),
            pltpu.VMEM((2, 2, 128, 128), F32),
            pltpu.VMEM((2, 128, 256), BF16),
            pltpu.VMEM((2, 2, 2, 128, 256), BF16),
            pltpu.VMEM((4, 128, 128), F32),
            pltpu.VMEM((16, 2, 16, 128), BF16),
            pltpu.VMEM((16, 2, 16, 128), BF16),
            pltpu.VMEM((512, 128), F32),
            pltpu.VMEM((8, 64, 128), BF16),
            pltpu.VMEM((8, 64, 128), BF16),
            dma((12,)), dma((2, 7)), dma((2, 7)), dma((16,)), dma((16,)), dma((2, 16)), dma((2, 16)), dma((2, 4)),
            dma((2, 4)), dma((16,)), dma((16,)), dma((7,)), dma((7,)), pltpu.SemaphoreType.REGULAR, pltpu.SemaphoreType.REGULAR,
            pltpu.SemaphoreType.REGULAR,
        ],
        compiler_params=pltpu.CompilerParams(collective_id=0, has_side_effects=True, vmem_limit_bytes=32 << 20),
        name="triangle",
    )(*[pltpu.with_memory_space_constraint(a, pltpu.HBM) for a in args])


def solution(mesh):
    return jax.shard_map(
        per_device,
        mesh=mesh,
        in_specs=(P("row", "col", None), P("row", "col")) + (P(),) * 10,
        out_specs=P("row", "col", None),
        check_vma=False,
    )
```

```python
import jax
import jax.numpy as jnp
from jax import lax
from jax.experimental import pallas as pl
from jax.experimental.pallas import tpu as pltpu
from jax.sharding import PartitionSpec as P

MESH = pl.DeviceIdType.MESH
F32, BF16 = jnp.float32, jnp.bfloat16
NZ, NX, NY = 16, 4, 4
FAR_FIRST = (8, 7, 9, 6, 10, 5, 11, 4, 12, 3, 13, 2, 14, 1, 15)
NEAR = (4, 12, 3, 13, 2, 14, 1, 15)
STEP = 14
EARLY = 1
ALONG_Y = (2, 1, 3)
X_AND_CORE = tuple((dx, dc) for dx in (2, 1, 3, 0) for dc in (1, 0) if dx or dc)
NT = (((1,), (1,)), ((), ()))
TN = (((0,), (0,)), ((), ()))


def swap_blocks(arrays):
    arrays = list(arrays)
    lane = lax.broadcasted_iota(jnp.int32, arrays[0].shape, 1)
    for bit in range(3):
        step = 1 << bit
        upper = ((lane // 16) // step) % 2 == 1
        for a in range(8):
            if not a & step:
                low, high = arrays[a], arrays[a | step]
                arrays[a] = jnp.where(upper, pltpu.roll(high, 16 * step, 1), low)
                arrays[a | step] = jnp.where(upper, high, pltpu.roll(low, 128 - 16 * step, 1))
    return arrays


def kernel(
    pair_hbm, mask_hbm, norm_gain_hbm, norm_bias_hbm, w_a_gate_hbm, w_a_proj_hbm, w_b_gate_hbm, w_b_proj_hbm,
    w_gate_hbm, out_gain_hbm, out_bias_hbm, w_out_hbm,
    out_ref,
    pair, mask, norm_gain, norm_bias, w_a_gate, w_a_proj, w_b_gate, w_b_proj, w_gate, out_gain, out_bias, w_out,
    normed, gate, x_send, x_recv, left_rows, right_rows, left_send, left_recv, right_send, right_recv, left_turned,
    right_turned, left, right_all, product, back_z_send, back_z_recv, back_rows, back_x_send, back_x_recv,
    in_sem, x_ss, x_rs, left_ss, left_rs, right_ss, right_rs, y_ss, y_rs, back_z_ss, back_z_rs, back_x_ss, back_x_rs,
    ring_sem, core_sem, wave_sem,
):
    row, col = lax.axis_index("row"), lax.axis_index("col")
    y, core = row // 4, row % 2
    x = ((row // 2) % 2) * 2 + col // 16
    z = col % 16

    def device(y, x, core, z):
        return {"row": y * 4 + (x // 2) * 2 + core, "col": (x % 2) * 16 + z}

    def slot_of(x, core):
        return (x // 2) * 4 + core * 2 + x % 2

    def slot_at(dx, dc):
        return slot_of((x + dx + NX) % NX, (core + dc) % 2)

    def remote(src, dst, ss, rs, to):
        return pltpu.make_async_remote_copy(
            src_ref=src, dst_ref=dst, send_sem=ss, recv_sem=rs, device_id=to, device_id_type=MESH
        )

    slot = slot_of(x, core)
    other_core = device(y, x, 1 - core, z)
    x_peers = [device(y, (x + dx) % NX, (core + dc) % 2, z) for dx, dc in X_AND_CORE]
    y_peers = [device((y + d) % NY, x, core, z) for d in ALONG_Y]
    barrier = pltpu.get_barrier_semaphore()
    peers = [device(y, x, core, (z + d) % NZ) for d in NEAR] + x_peers + y_peers
    for peer in peers:
        pl.semaphore_signal(barrier, inc=1, device_id=peer, device_id_type=MESH)

    loads = [
        pltpu.make_async_copy(src, dst, in_sem.at[n])
        for n, (src, dst) in enumerate(
            (
                (pair_hbm, pair), (norm_gain_hbm, norm_gain), (norm_bias_hbm, norm_bias), (w_b_gate_hbm, w_b_gate),
                (w_b_proj_hbm, w_b_proj), (mask_hbm, mask), (w_a_gate_hbm, w_a_gate), (w_a_proj_hbm, w_a_proj),
                (w_gate_hbm, w_gate), (out_gain_hbm, out_gain), (out_bias_hbm, out_bias), (w_out_hbm, w_out),
            )
        )
    ]
    for load in loads:
        load.start()
    for load in loads[:3]:
        load.wait()

    values = pair[...].astype(F32).reshape(512, 128)
    centred = values - jnp.mean(values, axis=1, keepdims=True)
    variance = jnp.mean(centred * centred, axis=1, keepdims=True)
    normed[...] = (centred * lax.rsqrt(variance + 1e-05) * norm_gain[...] + norm_bias[...]).astype(BF16)

    for load in loads[3:6]:
        load.wait()

    at_col = lax.broadcasted_iota(jnp.int32, (16, 512), 1) % 16 == lax.broadcasted_iota(jnp.int32, (16, 512), 0)
    at_row = lax.broadcasted_iota(jnp.int32, (32, 512), 1) // 16 == lax.broadcasted_iota(jnp.int32, (32, 512), 0)
    spread = lax.dot_general(
        mask[...].astype(F32).astype(BF16), at_col.astype(F32).astype(BF16), TN, preferred_element_type=F32
    )
    mask_row = jnp.sum(jnp.where(at_row, spread, 0.0), axis=0, keepdims=True)

    def project(weight):
        turned_weight = weight[...].astype(F32).T.astype(BF16)
        return lax.dot_general(turned_weight, normed[...], NT, preferred_element_type=F32)

    def edges_of(side, w_gate, w_proj):
        edges = mask_row * jax.nn.sigmoid(project(w_gate)) * project(w_proj)
        x_send[side] = edges.reshape(8, 16, 512).astype(BF16)

    def start_along_x(side):
        for n, (dx, dc) in enumerate(X_AND_CORE):
            remote(
                x_send.at[side, slot_at(dx, dc)], x_recv.at[side, slot], x_ss.at[side, n], x_rs.at[side, n], x_peers[n]
            ).start()
        x_recv[side, slot] = x_send[side, slot]

    def wait_along_x(side, first_slot, slots):
        for n, (dx, dc) in enumerate(X_AND_CORE):
            source = slot_at(-dx, dc)

            def wait():
                remote(
                    x_send.at[side, 0], x_recv.at[side, source], x_ss.at[side, n], x_rs.at[side, n], other_core
                ).wait_recv()

            if slots == 8:
                wait()
            else:
                pl.when(source // 4 == first_slot // 4)(wait)

    def start_along_z(send, recv, ss, rs):
        for d in FAR_FIRST:
            remote(send.at[(z + d) % NZ], recv.at[d], ss.at[d], rs.at[d], device(y, x, core, (z + d) % NZ)).start()
        recv[0] = send[z]

    def finish_along_z(send, recv, ss, rs, turned, slots):
        for d in FAR_FIRST:
            remote(send.at[0], recv.at[d], ss.at[d], rs.at[d], other_core).wait_recv()
        count = 4 * slots
        for half in range(2):
            blocks = swap_blocks([recv[half * 8 + a].astype(F32) for a in range(8)])
            for low in range(8):
                turned[half, low * count : low * count + count, :] = blocks[low]
        result = []
        for x_low in range(2):
            halves = []
            for half in range(2):
                starts = [part * slots + s for s in range(x_low, slots, 2) for part in range(4)]
                rows = [turned[half, pl.ds(start, 8, stride=count), :] for start in starts]
                halves.append(jnp.concatenate(rows, axis=0))
            result.append(jnp.concatenate(halves, axis=1).astype(BF16))
        return result

    def by_plane(side, first_slot, slots, rows, send):
        wait_along_x(side, first_slot, slots)
        for part in range(4):
            lanes = slice(part * 128, part * 128 + 128)
            block = x_recv[side, first_slot : first_slot + slots, :, lanes].astype(F32).reshape(slots * 16, 128)
            rows[part * slots * 16 : (part + 1) * slots * 16, :] = block
        for plane in range(NZ):
            send[plane] = rows[pl.ds(plane, 4 * slots, stride=16), :].astype(BF16)

    left_z = (left_send, left_recv, left_ss, left_rs)
    right_z = [(right_send.at[h], right_recv.at[h], right_ss.at[h], right_rs.at[h]) for h in range(2)]

    def send_left():
        by_plane(0, 0, 8, left_rows, left_send)
        start_along_z(*left_z)

    def send_right(h):
        by_plane(1, h * 4, 4, right_rows.at[h], right_send.at[h])
        start_along_z(*right_z[h])

    edges_of(1, w_b_gate, w_b_proj)
    pl.semaphore_wait(barrier, len(peers))
    for d in (4, 12):
        pl.semaphore_signal(ring_sem, inc=1, device_id=device(y, x, core, (z + d) % NZ), device_id_type=MESH)
    start_along_x(1)
    for load in loads[6:]:
        load.wait()
    edges_of(0, w_a_gate, w_a_proj)
    pl.semaphore_wait(ring_sem, 2)

    def wait_sent(send, recv, ss, rs, distances):
        for d in distances:
            remote(send.at[0], recv.at[d], ss.at[d], rs.at[d], other_core).wait_send()

    def after_both_cores(send, recv, ss, rs):
        d = FAR_FIRST[STEP]
        remote(send.at[0], recv.at[d], ss.at[d], rs.at[d], other_core).wait_send()
        pl.semaphore_signal(core_sem, inc=1, device_id=other_core, device_id_type=MESH)
        pl.semaphore_wait(core_sem, 1)

    send_right(0)
    start_along_x(0)
    send_right(1)
    after_both_cores(*right_z[0])
    send_left()
    gate[...] = jax.nn.sigmoid(jnp.dot(normed[...], w_gate[...], preferred_element_type=F32))

    def right_of(of_y, h):
        return right_all.at[of_y % 2, h, :, pl.ds(pl.multiple_of((of_y // 2) * 64, 64), 64), :]

    def y_copy(h, d, of_y):
        return remote(right_of(y, h), right_of(of_y, h), y_ss.at[h, d], y_rs.at[h, d], device((y + d) % NY, x, core, z))

    def send_along_y(h):
        for x_low, rows in enumerate(finish_along_z(*right_z[h], right_turned.at[h], 4)):
            right_all[y % 2, h, x_low, pl.ds(pl.multiple_of((y // 2) * 64, 64), 64), :] = rows
        for d in ALONG_Y:
            y_copy(h, d, y).start()

    def back_z_copy(to_z):
        return remote(
            back_z_send.at[to_z], back_z_recv.at[z], back_z_ss.at[to_z], back_z_rs.at[z], device(y, x, core, to_z)
        )

    def wait_along_y(odd, h):
        for of_y in (odd, odd + 2):
            d = (y + NY - of_y) % NY

            @pl.when(d != 0)
            def _():
                y_copy(h, d, of_y).wait_recv()

    def contract(odd, h):
        if odd or h:
            wait_along_y(odd, h)
        product[odd * 2 + h] = lax.dot_general(
            left[0], right_all[odd, h, 0], NT, preferred_element_type=F32
        ) + lax.dot_general(left[1], right_all[odd, h, 1], NT, preferred_element_type=F32)
        blocks = swap_blocks([product[odd * 2 + h, pl.ds(low, 16, stride=8), :] for low in range(8)])
        for low in range(8):
            back_z_send[odd * 8 + h * 4 + low % 4, low // 4] = blocks[low].astype(BF16)
        for to_z in range(odd * 8 + h * 4, odd * 8 + h * 4 + 4):

            @pl.when(z != to_z)
            def _():
                back_z_copy(to_z).start()

    @pl.when(y % 2 == 0)
    def _():
        send_along_y(0)
        send_along_y(1)

    wait_along_y(0, 0)

    @pl.when(y % 2 == 1)
    def _():
        send_along_y(0)
        send_along_y(1)

    for x_low, rows in enumerate(finish_along_z(*left_z, left_turned, 8)):
        left[x_low] = rows
    contract(0, 0)

    first = jnp.where(z == 0, 1, 0)
    back_z_copy(first).wait_send()
    pl.semaphore_signal(wave_sem, inc=1, device_id=other_core, device_id_type=MESH)
    pl.semaphore_wait(wave_sem, 1)
    contract(0, 1)

    def contract_high():
        contract(1, 0)
        contract(1, 1)

    pl.when(z >= EARLY)(contract_high)
    for side in range(2):
        for n in range(len(X_AND_CORE)):
            remote(
                x_send.at[side, 0], x_recv.at[side, 0], x_ss.at[side, n], x_rs.at[side, n], other_core
            ).wait_send()
    wait_sent(*left_z, FAR_FIRST)
    wait_sent(*right_z[1], FAR_FIRST)
    wait_sent(*right_z[0], FAR_FIRST[:STEP] + FAR_FIRST[STEP + 1 :])
    for h in range(2):
        for d in ALONG_Y:
            y_copy(h, d, y).wait_send()

    back_z_recv[z] = back_z_send[z]
    for d in FAR_FIRST:
        from_z = (z + NZ - d) % NZ
        remote(
            back_z_send.at[0], back_z_recv.at[from_z], back_z_ss.at[from_z], back_z_rs.at[from_z], other_core
        ).wait_recv()

    back_rows[...] = back_z_recv[...].astype(F32).reshape(512, 128)
    for to_core in range(2):
        for to_x in range(NX):
            start = (to_x % 2) * 16 + (to_x // 2) * 8 + to_core * 4
            rows = [back_rows[pl.ds(start + part, 16, stride=32), :] for part in range(4)]
            back_x_send[slot_of(to_x, to_core)] = jnp.concatenate(rows, axis=0).astype(BF16)
    back_x = [
        remote(back_x_send.at[slot_at(dx, dc)], back_x_recv.at[slot], back_x_ss.at[n], back_x_rs.at[n], x_peers[n])
        for n, (dx, dc) in enumerate(X_AND_CORE)
    ]
    for copy in back_x:
        copy.start()
    gain_col = jnp.broadcast_to(out_gain[...], (8, 128)).T[:, :1]
    bias_col = jnp.broadcast_to(out_bias[...], (8, 128)).T[:, :1]
    back_x_recv[slot] = back_x_send[slot]
    pl.when(z < EARLY)(contract_high)
    for d in FAR_FIRST:
        to_z = (z + d) % NZ
        pl.when(to_z != first)(lambda: back_z_copy(to_z).wait_send())
    for n, (dx, dc) in enumerate(X_AND_CORE):
        arrived = back_x_recv.at[slot_at(-dx, dc)]
        remote(back_x_send.at[0], arrived, back_x_ss.at[n], back_x_rs.at[n], x_peers[n]).wait_recv()

    for part in range(4):
        contracted = back_x_recv[:, part * 16 : part * 16 + 16, :].astype(F32).reshape(128, 128)
        centred = contracted - jnp.mean(contracted, axis=0, keepdims=True)
        variance = jnp.mean(centred * centred, axis=0, keepdims=True)
        normed_out = (centred * lax.rsqrt(variance + 1e-05) * gain_col + bias_col).T.astype(BF16)
        result = gate[part * 128 : part * 128 + 128, :] * jnp.dot(normed_out, w_out[...], preferred_element_type=F32)
        out_ref[part * 8 : part * 8 + 8] = result.astype(BF16).reshape(8, 16, 128)

    for copy in back_x:
        copy.wait_send()


def per_device(
    pair, pair_mask, norm_gain, norm_bias, w_a_gate, w_a_proj, w_b_gate, w_b_proj, w_gate, out_gain, out_bias, w_out
):
    args = (
        pair, pair_mask.T, norm_gain.reshape(1, 128), norm_bias.reshape(1, 128), w_a_gate, w_a_proj, w_b_gate, w_b_proj,
        w_gate, out_gain.reshape(1, 128), out_bias.reshape(1, 128), w_out,
    )
    dma = pltpu.SemaphoreType.DMA
    return pl.pallas_call(
        kernel,
        out_shape=pltpu.VMEM(pair.shape, BF16),
        in_specs=[pl.BlockSpec(memory_space=pl.ANY)] * len(args),
        out_specs=pl.BlockSpec(memory_space=pltpu.VMEM),
        scratch_shapes=[pltpu.VMEM(a.shape, a.dtype) for a in args]
        + [
            pltpu.VMEM((512, 128), BF16),
            pltpu.VMEM((512, 128), F32),
            pltpu.VMEM((2, 8, 16, 512), BF16),
            pltpu.VMEM((2, 8, 16, 512), BF16),
            pltpu.VMEM((512, 128), F32),
            pltpu.VMEM((2, 256, 128), F32),
            pltpu.VMEM((16, 32, 128), BF16),
            pltpu.VMEM((16, 32, 128), BF16),
            pltpu.VMEM((2, 16, 16, 128), BF16),
            pltpu.VMEM((2, 16, 16, 128), BF16),
            pltpu.VMEM((2, 256, 128), F32),
            pltpu.VMEM((2, 2, 128, 128), F32),
            pltpu.VMEM((2, 128, 256), BF16),
            pltpu.VMEM((2, 2, 2, 128, 256), BF16),
            pltpu.VMEM((4, 128, 128), F32),
            pltpu.VMEM((16, 2, 16, 128), BF16),
            pltpu.VMEM((16, 2, 16, 128), BF16),
            pltpu.VMEM((512, 128), F32),
            pltpu.VMEM((8, 64, 128), BF16),
            pltpu.VMEM((8, 64, 128), BF16),
            dma((12,)), dma((2, 7)), dma((2, 7)), dma((16,)), dma((16,)), dma((2, 16)), dma((2, 16)), dma((2, 4)),
            dma((2, 4)), dma((16,)), dma((16,)), dma((7,)), dma((7,)), pltpu.SemaphoreType.REGULAR, pltpu.SemaphoreType.REGULAR,
            pltpu.SemaphoreType.REGULAR,
        ],
        compiler_params=pltpu.CompilerParams(collective_id=0, has_side_effects=True, vmem_limit_bytes=32 << 20),
        name="triangle",
    )(*[pltpu.with_memory_space_constraint(a, pltpu.HBM) for a in args])


def solution(mesh):
    return jax.shard_map(
        per_device,
        mesh=mesh,
        in_specs=(P("row", "col", None), P("row", "col")) + (P(),) * 10,
        out_specs=P("row", "col", None),
        check_vma=False,
    )
```

```python
import jax
import jax.numpy as jnp
from jax import lax
from jax.experimental import pallas as pl
from jax.experimental.pallas import tpu as pltpu
from jax.sharding import PartitionSpec as P

MESH = pl.DeviceIdType.MESH
F32, BF16 = jnp.float32, jnp.bfloat16
NZ, NX, NY = 16, 4, 4
FAR_FIRST = (8, 7, 9, 6, 10, 5, 11, 4, 12, 3, 13, 2, 14, 1, 15)
NEAR = (4, 12, 3, 13, 2, 14, 1, 15)
STEP = 6
EARLY = 1
ALONG_Y = (2, 1, 3)
X_AND_CORE = tuple((dx, dc) for dx in (2, 1, 3, 0) for dc in (1, 0) if dx or dc)
NT = (((1,), (1,)), ((), ()))
TN = (((0,), (0,)), ((), ()))


def swap_blocks(arrays):
    arrays = list(arrays)
    lane = lax.broadcasted_iota(jnp.int32, arrays[0].shape, 1)
    for bit in range(3):
        step = 1 << bit
        upper = ((lane // 16) // step) % 2 == 1
        for a in range(8):
            if not a & step:
                low, high = arrays[a], arrays[a | step]
                arrays[a] = jnp.where(upper, pltpu.roll(high, 16 * step, 1), low)
                arrays[a | step] = jnp.where(upper, high, pltpu.roll(low, 128 - 16 * step, 1))
    return arrays


def kernel(
    pair_hbm, mask_hbm, norm_gain_hbm, norm_bias_hbm, w_a_gate_hbm, w_a_proj_hbm, w_b_gate_hbm, w_b_proj_hbm,
    w_gate_hbm, out_gain_hbm, out_bias_hbm, w_out_hbm,
    out_ref,
    pair, mask, norm_gain, norm_bias, w_a_gate, w_a_proj, w_b_gate, w_b_proj, w_gate, out_gain, out_bias, w_out,
    normed, gate, x_send, x_recv, left_rows, right_rows, left_send, left_recv, right_send, right_recv, left_turned,
    right_turned, left, right_all, product, back_z_send, back_z_recv, back_rows, back_x_send, back_x_recv,
    in_sem, x_ss, x_rs, left_ss, left_rs, right_ss, right_rs, y_ss, y_rs, back_z_ss, back_z_rs, back_x_ss, back_x_rs,
    ring_sem, core_sem, wave_sem,
):
    row, col = lax.axis_index("row"), lax.axis_index("col")
    y, core = row // 4, row % 2
    x = ((row // 2) % 2) * 2 + col // 16
    z = col % 16

    def device(y, x, core, z):
        return {"row": y * 4 + (x // 2) * 2 + core, "col": (x % 2) * 16 + z}

    def slot_of(x, core):
        return (x // 2) * 4 + core * 2 + x % 2

    def slot_at(dx, dc):
        return slot_of((x + dx + NX) % NX, (core + dc) % 2)

    def remote(src, dst, ss, rs, to):
        return pltpu.make_async_remote_copy(
            src_ref=src, dst_ref=dst, send_sem=ss, recv_sem=rs, device_id=to, device_id_type=MESH
        )

    slot = slot_of(x, core)
    other_core = device(y, x, 1 - core, z)
    x_peers = [device(y, (x + dx) % NX, (core + dc) % 2, z) for dx, dc in X_AND_CORE]
    y_peers = [device((y + d) % NY, x, core, z) for d in ALONG_Y]
    barrier = pltpu.get_barrier_semaphore()
    peers = [device(y, x, core, (z + d) % NZ) for d in NEAR] + x_peers + y_peers
    for peer in peers:
        pl.semaphore_signal(barrier, inc=1, device_id=peer, device_id_type=MESH)

    loads = [
        pltpu.make_async_copy(src, dst, in_sem.at[n])
        for n, (src, dst) in enumerate(
            (
                (pair_hbm, pair), (norm_gain_hbm, norm_gain), (norm_bias_hbm, norm_bias), (w_b_gate_hbm, w_b_gate),
                (w_b_proj_hbm, w_b_proj), (mask_hbm, mask), (w_a_gate_hbm, w_a_gate), (w_a_proj_hbm, w_a_proj),
                (w_gate_hbm, w_gate), (out_gain_hbm, out_gain), (out_bias_hbm, out_bias), (w_out_hbm, w_out),
            )
        )
    ]
    for load in loads:
        load.start()
    for load in loads[:3]:
        load.wait()

    values = pair[...].astype(F32).reshape(512, 128)
    centred = values - jnp.mean(values, axis=1, keepdims=True)
    variance = jnp.mean(centred * centred, axis=1, keepdims=True)
    normed[...] = (centred * lax.rsqrt(variance + 1e-05) * norm_gain[...] + norm_bias[...]).astype(BF16)

    for load in loads[3:6]:
        load.wait()

    at_col = lax.broadcasted_iota(jnp.int32, (16, 512), 1) % 16 == lax.broadcasted_iota(jnp.int32, (16, 512), 0)
    at_row = lax.broadcasted_iota(jnp.int32, (32, 512), 1) // 16 == lax.broadcasted_iota(jnp.int32, (32, 512), 0)
    spread = lax.dot_general(
        mask[...].astype(F32).astype(BF16), at_col.astype(F32).astype(BF16), TN, preferred_element_type=F32
    )
    mask_row = jnp.sum(jnp.where(at_row, spread, 0.0), axis=0, keepdims=True)

    def project(weight):
        turned_weight = weight[...].astype(F32).T.astype(BF16)
        return lax.dot_general(turned_weight, normed[...], NT, preferred_element_type=F32)

    def edges_of(side, w_gate, w_proj):
        edges = mask_row * jax.nn.sigmoid(project(w_gate)) * project(w_proj)
        x_send[side] = edges.reshape(8, 16, 512).astype(BF16)

    def start_along_x(side):
        for n, (dx, dc) in enumerate(X_AND_CORE):
            remote(
                x_send.at[side, slot_at(dx, dc)], x_recv.at[side, slot], x_ss.at[side, n], x_rs.at[side, n], x_peers[n]
            ).start()
        x_recv[side, slot] = x_send[side, slot]

    def wait_along_x(side, first_slot, slots):
        for n, (dx, dc) in enumerate(X_AND_CORE):
            source = slot_at(-dx, dc)

            def wait():
                remote(
                    x_send.at[side, 0], x_recv.at[side, source], x_ss.at[side, n], x_rs.at[side, n], other_core
                ).wait_recv()

            if slots == 8:
                wait()
            else:
                pl.when(source // 4 == first_slot // 4)(wait)

    def start_along_z(send, recv, ss, rs):
        for d in FAR_FIRST:
            remote(send.at[(z + d) % NZ], recv.at[d], ss.at[d], rs.at[d], device(y, x, core, (z + d) % NZ)).start()
        recv[0] = send[z]

    def finish_along_z(send, recv, ss, rs, turned, slots):
        for d in FAR_FIRST:
            remote(send.at[0], recv.at[d], ss.at[d], rs.at[d], other_core).wait_recv()
        count = 4 * slots
        for half in range(2):
            blocks = swap_blocks([recv[half * 8 + a].astype(F32) for a in range(8)])
            for low in range(8):
                turned[half, low * count : low * count + count, :] = blocks[low]
        result = []
        for x_low in range(2):
            halves = []
            for half in range(2):
                starts = [part * slots + s for s in range(x_low, slots, 2) for part in range(4)]
                rows = [turned[half, pl.ds(start, 8, stride=count), :] for start in starts]
                halves.append(jnp.concatenate(rows, axis=0))
            result.append(jnp.concatenate(halves, axis=1).astype(BF16))
        return result

    def by_plane(side, first_slot, slots, rows, send):
        wait_along_x(side, first_slot, slots)
        for part in range(4):
            lanes = slice(part * 128, part * 128 + 128)
            block = x_recv[side, first_slot : first_slot + slots, :, lanes].astype(F32).reshape(slots * 16, 128)
            rows[part * slots * 16 : (part + 1) * slots * 16, :] = block
        for plane in range(NZ):
            send[plane] = rows[pl.ds(plane, 4 * slots, stride=16), :].astype(BF16)

    left_z = (left_send, left_recv, left_ss, left_rs)
    right_z = [(right_send.at[h], right_recv.at[h], right_ss.at[h], right_rs.at[h]) for h in range(2)]

    def send_left():
        by_plane(0, 0, 8, left_rows, left_send)
        start_along_z(*left_z)

    def send_right(h):
        by_plane(1, h * 4, 4, right_rows.at[h], right_send.at[h])
        start_along_z(*right_z[h])

    edges_of(1, w_b_gate, w_b_proj)
    pl.semaphore_wait(barrier, len(peers))
    for d in (4, 12):
        pl.semaphore_signal(ring_sem, inc=1, device_id=device(y, x, core, (z + d) % NZ), device_id_type=MESH)
    start_along_x(1)
    for load in loads[6:]:
        load.wait()
    edges_of(0, w_a_gate, w_a_proj)
    pl.semaphore_wait(ring_sem, 2)

    def wait_sent(send, recv, ss, rs, distances):
        for d in distances:
            remote(send.at[0], recv.at[d], ss.at[d], rs.at[d], other_core).wait_send()

    def after_both_cores(send, recv, ss, rs):
        d = FAR_FIRST[STEP]
        remote(send.at[0], recv.at[d], ss.at[d], rs.at[d], other_core).wait_send()
        pl.semaphore_signal(core_sem, inc=1, device_id=other_core, device_id_type=MESH)
        pl.semaphore_wait(core_sem, 1)

    send_right(0)
    start_along_x(0)
    send_right(1)
    after_both_cores(*right_z[0])
    send_left()
    gate[...] = jax.nn.sigmoid(jnp.dot(normed[...], w_gate[...], preferred_element_type=F32))

    def right_of(of_y, h):
        return right_all.at[of_y % 2, h, :, pl.ds(pl.multiple_of((of_y // 2) * 64, 64), 64), :]

    def y_copy(h, d, of_y):
        return remote(right_of(y, h), right_of(of_y, h), y_ss.at[h, d], y_rs.at[h, d], device((y + d) % NY, x, core, z))

    def send_along_y(h):
        for x_low, rows in enumerate(finish_along_z(*right_z[h], right_turned.at[h], 4)):
            right_all[y % 2, h, x_low, pl.ds(pl.multiple_of((y // 2) * 64, 64), 64), :] = rows
        for d in ALONG_Y:
            y_copy(h, d, y).start()

    def back_z_copy(to_z):
        return remote(
            back_z_send.at[to_z], back_z_recv.at[z], back_z_ss.at[to_z], back_z_rs.at[z], device(y, x, core, to_z)
        )

    def wait_along_y(odd, h):
        for of_y in (odd, odd + 2):
            d = (y + NY - of_y) % NY

            @pl.when(d != 0)
            def _():
                y_copy(h, d, of_y).wait_recv()

    def contract(odd, h):
        if odd or h:
            wait_along_y(odd, h)
        product[odd * 2 + h] = lax.dot_general(
            left[0], right_all[odd, h, 0], NT, preferred_element_type=F32
        ) + lax.dot_general(left[1], right_all[odd, h, 1], NT, preferred_element_type=F32)
        blocks = swap_blocks([product[odd * 2 + h, pl.ds(low, 16, stride=8), :] for low in range(8)])
        for low in range(8):
            back_z_send[odd * 8 + h * 4 + low % 4, low // 4] = blocks[low].astype(BF16)
        for to_z in range(odd * 8 + h * 4, odd * 8 + h * 4 + 4):

            @pl.when(z != to_z)
            def _():
                back_z_copy(to_z).start()

    @pl.when(y % 2 == 0)
    def _():
        send_along_y(0)
        send_along_y(1)

    wait_along_y(0, 0)

    @pl.when(y % 2 == 1)
    def _():
        send_along_y(0)
        send_along_y(1)

    for x_low, rows in enumerate(finish_along_z(*left_z, left_turned, 8)):
        left[x_low] = rows
    contract(0, 0)

    first = jnp.where(z == 0, 1, 0)
    back_z_copy(first).wait_send()
    pl.semaphore_signal(wave_sem, inc=1, device_id=other_core, device_id_type=MESH)
    pl.semaphore_wait(wave_sem, 1)
    contract(0, 1)

    def contract_high():
        contract(1, 0)
        contract(1, 1)

    pl.when(z >= EARLY)(contract_high)
    for side in range(2):
        for n in range(len(X_AND_CORE)):
            remote(
                x_send.at[side, 0], x_recv.at[side, 0], x_ss.at[side, n], x_rs.at[side, n], other_core
            ).wait_send()
    wait_sent(*left_z, FAR_FIRST)
    wait_sent(*right_z[1], FAR_FIRST)
    wait_sent(*right_z[0], FAR_FIRST[:STEP] + FAR_FIRST[STEP + 1 :])
    for h in range(2):
        for d in ALONG_Y:
            y_copy(h, d, y).wait_send()

    back_z_recv[z] = back_z_send[z]
    for d in FAR_FIRST:
        from_z = (z + NZ - d) % NZ
        remote(
            back_z_send.at[0], back_z_recv.at[from_z], back_z_ss.at[from_z], back_z_rs.at[from_z], other_core
        ).wait_recv()

    back_rows[...] = back_z_recv[...].astype(F32).reshape(512, 128)
    for to_core in range(2):
        for to_x in range(NX):
            start = (to_x % 2) * 16 + (to_x // 2) * 8 + to_core * 4
            rows = [back_rows[pl.ds(start + part, 16, stride=32), :] for part in range(4)]
            back_x_send[slot_of(to_x, to_core)] = jnp.concatenate(rows, axis=0).astype(BF16)
    back_x = [
        remote(back_x_send.at[slot_at(dx, dc)], back_x_recv.at[slot], back_x_ss.at[n], back_x_rs.at[n], x_peers[n])
        for n, (dx, dc) in enumerate(X_AND_CORE)
    ]
    for copy in back_x:
        copy.start()
    gain_col = jnp.broadcast_to(out_gain[...], (8, 128)).T[:, :1]
    bias_col = jnp.broadcast_to(out_bias[...], (8, 128)).T[:, :1]
    back_x_recv[slot] = back_x_send[slot]
    pl.when(z < EARLY)(contract_high)
    for d in FAR_FIRST:
        to_z = (z + d) % NZ
        pl.when(to_z != first)(lambda: back_z_copy(to_z).wait_send())
    for n, (dx, dc) in enumerate(X_AND_CORE):
        arrived = back_x_recv.at[slot_at(-dx, dc)]
        remote(back_x_send.at[0], arrived, back_x_ss.at[n], back_x_rs.at[n], x_peers[n]).wait_recv()

    for part in range(4):
        contracted = back_x_recv[:, part * 16 : part * 16 + 16, :].astype(F32).reshape(128, 128)
        centred = contracted - jnp.mean(contracted, axis=0, keepdims=True)
        variance = jnp.mean(centred * centred, axis=0, keepdims=True)
        normed_out = (centred * lax.rsqrt(variance + 1e-05) * gain_col + bias_col).T.astype(BF16)
        result = gate[part * 128 : part * 128 + 128, :] * jnp.dot(normed_out, w_out[...], preferred_element_type=F32)
        out_ref[part * 8 : part * 8 + 8] = result.astype(BF16).reshape(8, 16, 128)

    for copy in back_x:
        copy.wait_send()


def per_device(
    pair, pair_mask, norm_gain, norm_bias, w_a_gate, w_a_proj, w_b_gate, w_b_proj, w_gate, out_gain, out_bias, w_out
):
    args = (
        pair, pair_mask.T, norm_gain.reshape(1, 128), norm_bias.reshape(1, 128), w_a_gate, w_a_proj, w_b_gate, w_b_proj,
        w_gate, out_gain.reshape(1, 128), out_bias.reshape(1, 128), w_out,
    )
    dma = pltpu.SemaphoreType.DMA
    return pl.pallas_call(
        kernel,
        out_shape=pltpu.VMEM(pair.shape, BF16),
        in_specs=[pl.BlockSpec(memory_space=pl.ANY)] * len(args),
        out_specs=pl.BlockSpec(memory_space=pltpu.VMEM),
        scratch_shapes=[pltpu.VMEM(a.shape, a.dtype) for a in args]
        + [
            pltpu.VMEM((512, 128), BF16),
            pltpu.VMEM((512, 128), F32),
            pltpu.VMEM((2, 8, 16, 512), BF16),
            pltpu.VMEM((2, 8, 16, 512), BF16),
            pltpu.VMEM((512, 128), F32),
            pltpu.VMEM((2, 256, 128), F32),
            pltpu.VMEM((16, 32, 128), BF16),
            pltpu.VMEM((16, 32, 128), BF16),
            pltpu.VMEM((2, 16, 16, 128), BF16),
            pltpu.VMEM((2, 16, 16, 128), BF16),
            pltpu.VMEM((2, 256, 128), F32),
            pltpu.VMEM((2, 2, 128, 128), F32),
            pltpu.VMEM((2, 128, 256), BF16),
            pltpu.VMEM((2, 2, 2, 128, 256), BF16),
            pltpu.VMEM((4, 128, 128), F32),
            pltpu.VMEM((16, 2, 16, 128), BF16),
            pltpu.VMEM((16, 2, 16, 128), BF16),
            pltpu.VMEM((512, 128), F32),
            pltpu.VMEM((8, 64, 128), BF16),
            pltpu.VMEM((8, 64, 128), BF16),
            dma((12,)), dma((2, 7)), dma((2, 7)), dma((16,)), dma((16,)), dma((2, 16)), dma((2, 16)), dma((2, 4)),
            dma((2, 4)), dma((16,)), dma((16,)), dma((7,)), dma((7,)), pltpu.SemaphoreType.REGULAR, pltpu.SemaphoreType.REGULAR,
            pltpu.SemaphoreType.REGULAR,
        ],
        compiler_params=pltpu.CompilerParams(collective_id=0, has_side_effects=True, vmem_limit_bytes=32 << 20),
        name="triangle",
    )(*[pltpu.with_memory_space_constraint(a, pltpu.HBM) for a in args])


def solution(mesh):
    return jax.shard_map(
        per_device,
        mesh=mesh,
        in_specs=(P("row", "col", None), P("row", "col")) + (P(),) * 10,
        out_specs=P("row", "col", None),
        check_vma=False,
    )
```
